256 devices in a mesh: band: 16 (over z, core), lev: 16 (over y, x).
Axes of the slice: x: 4, y: 4, z: 8, core: 2. Of those that a mesh axis runs over, the one named last changes fastest.
Arguments:
- spectral: bfloat16 [256, 2, 320, 641], P('lev', None, 'band'), may hold values from -0.29882812 to 0.29882812
- legendre: bfloat16 [320, 128, 641], P('band'), may hold values from -0.3125 to 0.3125
- weights: float32 [128], replicated, may hold values from 2 to 40
- vertical: bfloat16 [256, 256], replicated, may hold values from -0.375 to 0.375
- grid_factor: bfloat16 [256, 2688], P('band'), may hold values from 0.29882812 to 3
- points: int32 [128], replicated, may hold values from 20 to 2576, as said below
- cutoffs: int32 [128], replicated, may hold values from 6 to 639, as said below
- row_latitude: int32 [256], replicated, may hold values from 0 to 255, each once
- slot_pair: int32 [320], replicated, may hold values from 0 to 319, each once
Outputs:
- grid_field: bfloat16 [256, 256, 2688], P('band', 'lev')
- round_trip: float32 [256, 2, 320, 641], P('lev', None, 'band')
The draws below stay inside these ranges and needn't reach their ends.
Inputs may be any that keep to these rules, and one draw needn't show every extreme that they name: points: 4 r + 16 for a cycle number r of 1 to 640; some latitude has 2576 points. cutoffs: at most min(639, (points - 1) // 2) of the same latitude; some latitude keeps 639. `row_latitude`: a permutation; latitudes below 128 are northern, latitude 128 + j mirrors j. `slot_pair`: a permutation; pair k joins wavenumbers k and 639 - k.
All inputs are finite; a program needn't handle non-finite values.
Results may differ from the reference program's by a relative error of at most 0.008.
Values may be sent and summed in bfloat16 or wider, within the bound.
No kernel may reach another device: no remote copies, remote signals or barrier semaphores. Data moves between devices by JAX's collectives and lax.ppermute only.
A program may use at most 128 MiB of HBM per device.

```python
import math
import jax
import jax.numpy as jnp
from jax import lax

PAIRS = 320
TRUNC = 639
COEFS = 641
LATS = 256
NORTH = 128
LEVELS = 256
PTS = 2688


def cycle_numbers(key):
    cycle_index = jax.random.randint(key, (NORTH,), 1, TRUNC + 2, dtype=jnp.int32)
    return cycle_index.at[0].set(TRUNC + 1)


def draw_points(key, part):
    cycle_index = cycle_numbers(key)
    return 4 * cycle_index + 16


def draw_cutoffs(key, part):
    cycle_index = cycle_numbers(key)
    key = jax.random.fold_in(key, 7)
    reduction = jax.random.randint(key, (NORTH,), 0, 4, dtype=jnp.int32)
    ceiling = jnp.minimum(TRUNC, 2 * cycle_index + 7) - reduction
    return ceiling.at[0].set(TRUNC)


def levels(own_key, extent, cuts, least, top_value):
    loudness = 1.0
    for dim, shards_of in cuts:
        heights = jax.random.uniform(jax.random.fold_in(jax.random.fold_in(own_key, 6), dim), (shards_of,), jnp.float32, least / len(cuts), top_value / len(cuts))
        loudness = loudness * jnp.repeat(jnp.exp(heights), extent[dim] // shards_of).reshape((-1,) + (1,) * (len(extent) - 1 - dim))
    return loudness


def bell_draw(stream_key, extent, deviation, most, shards=(), kind=jnp.bfloat16):
    gain = levels(stream_key, extent, shards, -0.22, 0.18) if shards else 1.0
    result = jax.random.normal(stream_key, extent, jnp.float32) * deviation * gain
    return jnp.minimum(jnp.maximum(result, -most), most).astype(kind)


def setup_inputs(seed: int = 0) -> dict:
    splits = jax.random.split(jax.random.key(seed), 10)
    spectral = bell_draw(splits[0], (LEVELS, 2, PAIRS, COEFS), 0.05, 0.29882812, ((0, 16), (2, 16)))
    legendre = bell_draw(splits[1], (PAIRS, NORTH, COEFS), (COEFS // 2) ** -0.5, 0.3125, ((0, 16),))
    weights = jnp.clip(jnp.exp(jax.random.uniform(splits[2], (NORTH,), jnp.float32, math.log(2.0), math.log(40.0))), 2.0, 40.0)
    vertical = bell_draw(splits[3], (LEVELS, LEVELS), LEVELS ** -0.5, 0.375)
    grid_factor = jnp.clip(jnp.exp(math.log(3.0) - 2.306499 * jax.random.uniform(splits[4], (LATS, PTS), jnp.float32) ** levels(splits[4], (LATS, PTS), ((0, 16),), -0.2, 0.2)), 0.29882812, 3.0).astype(jnp.bfloat16)
    points = draw_points(jax.random.fold_in(splits[9], 71), 0)
    cutoffs = draw_cutoffs(jax.random.fold_in(splits[9], 71), 0)
    row_latitude = jax.random.permutation(splits[7], LATS).astype(jnp.int32)
    slot_pair = jax.random.permutation(splits[8], PAIRS).astype(jnp.int32)
    return {"spectral": spectral, "legendre": legendre, "weights": weights, "vertical": vertical, "grid_factor": grid_factor, "points": points, "cutoffs": cutoffs, "row_latitude": row_latitude, "slot_pair": slot_pair}


def class_masks(pair_ids, truncation, width):
    column = jnp.arange(width, dtype=jnp.int32)[None, :]
    split_at = (truncation + 1 - pair_ids)[:, None]
    first_part = column < split_at
    parity = jnp.where(first_part, column, column - split_at) % 2
    category = jnp.where(first_part, 0, 2) + parity
    return (category[None] == jnp.arange(4, dtype=jnp.int32)[:, None, None]).astype(jnp.float32)


def mirror_fold(legendre_sums):
    north_rows = jnp.stack([legendre_sums[0] + legendre_sums[1], legendre_sums[2] + legendre_sums[3]], 3)
    south_rows = jnp.stack([legendre_sums[0] - legendre_sums[1], legendre_sums[2] - legendre_sums[3]], 3)
    return jnp.concatenate([north_rows, south_rows], 0)


def paired_classes(placed, weights):
    half_count = weights.shape[0]
    north_rows = placed[:half_count].astype(jnp.float32)
    south_rows = placed[half_count:].astype(jnp.float32)
    weighting = weights[:, None, None, None, None]
    even_part = (north_rows + south_rows) * weighting
    odd_part = (north_rows - south_rows) * weighting
    return jnp.stack([even_part[:, :, :, 0], odd_part[:, :, :, 0], even_part[:, :, :, 1], odd_part[:, :, :, 1]], 0)


def phase_tables(wavenumbers, row_points, outer_count):
    inner_index = jnp.arange(128, dtype=jnp.int32)
    outer_index = jnp.arange(outer_count, dtype=jnp.int32)
    unit_angle = 2.0 * math.pi / row_points.astype(jnp.float32)
    inner_angle = ((wavenumbers[:, None] * inner_index[None, :]) % row_points).astype(jnp.float32) * unit_angle
    outer_angle = ((wavenumbers[:, None] * (128 * outer_index)[None, :]) % row_points).astype(jnp.float32) * unit_angle
    return jnp.cos(inner_angle), jnp.sin(inner_angle), jnp.cos(outer_angle).T, jnp.sin(outer_angle).T


def inverse_row(fourier_row, row_points, row_cutoff, wavenumbers, row_width):
    outer_count = row_width // 128
    inner_cos, inner_sin, outer_cos, outer_sin = phase_tables(wavenumbers, row_points, outer_count)
    doubling = jnp.where(wavenumbers == 0, jnp.float32(1.0), jnp.float32(2.0))
    values = fourier_row.astype(jnp.float32) * (doubling * (wavenumbers <= row_cutoff).astype(jnp.float32))
    real_part = values[:, 0, None, :] * outer_cos[None] - values[:, 1, None, :] * outer_sin[None]
    imag_part = values[:, 0, None, :] * outer_sin[None] + values[:, 1, None, :] * outer_cos[None]
    twisted = jnp.concatenate([real_part, -imag_part], 2).astype(jnp.bfloat16)
    table = jnp.concatenate([inner_cos, inner_sin], 0).astype(jnp.bfloat16)
    samples = jnp.einsum("lqm,mp->lqp", twisted.astype(jnp.float32), table.astype(jnp.float32), precision=lax.Precision.HIGHEST)
    samples = samples.reshape(samples.shape[0], row_width)
    inside = jnp.arange(row_width, dtype=jnp.int32) < row_points
    return jnp.where(inside[None, :], samples, jnp.float32(0.0)).astype(jnp.bfloat16)


def direct_row(samples, row_points, row_cutoff, wavenumbers):
    level_total, row_width = samples.shape
    outer_count = row_width // 128
    inner_cos, inner_sin, outer_cos, outer_sin = phase_tables(wavenumbers, row_points, outer_count)
    table = jnp.concatenate([inner_cos, -inner_sin], 0).astype(jnp.bfloat16)
    blocks = samples.reshape(level_total, outer_count, 128)
    partial_sums = jnp.einsum("lqp,mp->lqm", blocks.astype(jnp.float32), table.astype(jnp.float32), precision=lax.Precision.HIGHEST)
    wave_total = wavenumbers.shape[0]
    cos_part = partial_sums[:, :, :wave_total]
    sin_part = partial_sums[:, :, wave_total:]
    real_sum = jnp.sum(cos_part * outer_cos[None] + sin_part * outer_sin[None], 1)
    imag_sum = jnp.sum(sin_part * outer_cos[None] - cos_part * outer_sin[None], 1)
    factor = (wavenumbers <= row_cutoff).astype(jnp.float32) / row_points.astype(jnp.float32)
    return (jnp.stack([real_sum, imag_sum], 1) * factor[None, None, :]).astype(jnp.bfloat16)


def reference(spectral, legendre, weights, vertical, grid_factor, points, cutoffs, row_latitude, slot_pair):
    selectors = class_masks(slot_pair, TRUNC, COEFS)
    masked = spectral[None] * selectors[:, None, None].astype(jnp.bfloat16)
    legendre_sums = jnp.einsum("qlrsc,sjc->qjlrs", masked.astype(jnp.float32), legendre.astype(jnp.float32), precision=lax.Precision.HIGHEST)
    by_latitude = mirror_fold(legendre_sums).astype(jnp.bfloat16)
    by_row = jnp.take(by_latitude, row_latitude, axis=0)
    fourier = by_row.reshape(LATS, LEVELS, 2, 2 * PAIRS)
    wavenumbers = jnp.concatenate([slot_pair, TRUNC - slot_pair])
    latitude_index = row_latitude % NORTH
    points_row = jnp.take(points, latitude_index)
    cutoff_row = jnp.take(cutoffs, latitude_index)
    vertical_wide = vertical.astype(jnp.float32)

    def transform_row(inputs):
        fourier_row, factor_row, row_points, row_cutoff = inputs
        grid_row = inverse_row(fourier_row, row_points, row_cutoff, wavenumbers, PTS)
        mixture = jnp.einsum("ak,kp->ap", vertical_wide, grid_row.astype(jnp.float32), precision=lax.Precision.HIGHEST)
        samples = (factor_row.astype(jnp.float32)[None, :] * mixture).astype(jnp.bfloat16)
        return grid_row, direct_row(samples, row_points, row_cutoff, wavenumbers)

    grid_field, harmonic = lax.map(transform_row, (fourier, grid_factor, points_row, cutoff_row))
    harmonic = harmonic.reshape(LATS, LEVELS, 2, 2, PAIRS)
    placed = jnp.zeros_like(harmonic).at[row_latitude].set(harmonic)
    parts = paired_classes(placed, weights).astype(jnp.bfloat16)
    projected = jnp.einsum("qjlrs,sjc->qlrsc", parts.astype(jnp.float32), legendre.astype(jnp.float32), precision=lax.Precision.HIGHEST)
    round_trip = jnp.sum(selectors[:, None, None] * projected, 0)
    return grid_field, round_trip
```

```python
import math

import jax
import jax.numpy as jnp
from jax import lax
from jax.experimental import pallas as pl
from jax.experimental.pallas import tpu as pltpu
from jax.sharding import PartitionSpec as P

F32, BF16 = jnp.float32, jnp.bfloat16
NB = 16
GROUPS = 5
WAVES = 1280
COS = (1.0, -19.739208221435547, 64.93938446044922, -85.45658111572266,
       60.241241455078125, -26.39919662475586, 7.783571243286133, -1.4335278272628784)
SIN = (6.2831854820251465, -41.34170150756836, 81.6052474975586, -76.70577239990234,
       42.05741882324219, -15.084507942199707, 3.775092124938965, -0.6134149432182312)
NT = (((1,), (1,)), ((), ()))


def params(limit=40):
    return pltpu.CompilerParams(vmem_limit_bytes=limit * 1024 * 1024)


def dot(a, b, dims=(((1,), (0,)), ((), ()))):
    return lax.dot_general(a, b, dims, preferred_element_type=F32)


def exchange_chunks(items, width):
    items = list(items)
    lane = lax.broadcasted_iota(jnp.int32, items[0][0].shape, 1)
    for level in range(4):
        step = 1 << level
        shift = width * step
        for low in range(16):
            if low & step:
                continue
            a, b = items[low], items[low + step]
            if shift == 128:
                items[low], items[low + step] = (a[0], b[0]), (a[1], b[1])
                continue
            keep = (lane & shift) == 0
            items[low] = tuple(jnp.where(keep, a[h], pltpu.roll(b[h], shift, 1)) for h in (0, 1))
            items[low + step] = tuple(
                jnp.where(keep, pltpu.roll(a[h], 128 - shift, 1), b[h]) for h in (0, 1)
            )
    return items


def swap_parts(x):
    lane = lax.broadcasted_iota(jnp.int32, (x.shape[0], 128), 1)
    even = (lane & 1) == 0
    pieces = []
    for t in range(x.shape[1] // 128):
        piece = x[:, 128 * t : 128 * (t + 1)]
        pieces.append(jnp.where(even, pltpu.roll(piece, 127, 1), pltpu.roll(piece, 1, 1)))
    return jnp.concatenate(pieces, 1)


def slot_columns(pair, width, truncation):
    column = lax.broadcasted_iota(jnp.int32, (1, width), 1)
    split = truncation + 1 - pair
    first = column < split
    odd = jnp.where(first, column, column - split) & 1
    return first, odd


def table_kernel(rows_per_step, band, row_latitude, points, waves, table, outer_cos, outer_sin, seeds):
    step = pl.program_id(0)
    wave = waves[...]
    imag = (lax.broadcasted_iota(jnp.int32, (1, WAVES), 1) & 1) == 1
    index = lax.broadcasted_iota(jnp.int32, (16, WAVES), 0).astype(F32)
    for r in range(rows_per_step):
        lat = row_latitude[band[0] * NB + step * rows_per_step + r] & (points.shape[0] - 1)
        count = jnp.full((1, WAVES), points[lat].astype(F32))
        inverse = 1.0 / count

        def circle(stride):
            product = (wave * stride) * index
            turns = jnp.floor(product * inverse + 0.5)
            y = (product - turns * count) * inverse
            z = y * y
            c = jnp.full_like(z, COS[-1])
            s = jnp.full_like(z, SIN[-1])
            for k in range(6, -1, -1):
                c = c * z + COS[k]
                s = s * z + SIN[k]
            return c, s * y

        c1, s1 = circle(1.0)
        c2, s2 = circle(16.0)
        seeds[0] = jnp.where(imag, s2, c2)
        seeds[1] = jnp.where(imag, -c2, s2)
        seeds[2] = c1
        seeds[3] = s1
        c3, s3 = circle(256.0)
        outer_cos[r] = c3
        outer_sin[r] = s3
        for t in range(5):
            lanes = slice(256 * t, 256 * (t + 1))
            c1, s1 = seeds[2, :, lanes], seeds[3, :, lanes]
            for a in range(16):
                value = seeds[0, a : a + 1, lanes] * c1 - seeds[1, a : a + 1, lanes] * s1
                table[r, 16 * a : 16 * (a + 1), lanes] = value.astype(BF16)


def send_kernel(truncation, band, slot_pair, lane_latitude, spectral, legendre, out, sums):
    group = pl.program_id(0)
    width = spectral.shape[-1]
    place = (
        lax.broadcasted_iota(jnp.int32, (256, 256), 0) == lane_latitude[...]
    ).astype(F32).astype(BF16)
    for s in range(4):
        first, odd = slot_columns(slot_pair[band[0] * 20 + group * 4 + s], width, truncation)
        one = first.astype(F32)
        sign = 1.0 - 2.0 * odd.astype(F32)
        x = spectral[s].reshape(32, width)
        picks = [one, 1.0 - one, one * sign, (1.0 - one) * sign]
        left = jnp.concatenate([x * p.astype(BF16) for p in picks], 0)
        values = dot(left, legendre[s]).astype(BF16)
        sums[64 * s : 64 * (s + 1), :128] = values[:64]
        sums[64 * s : 64 * (s + 1), 128:] = values[64:]
    placed = dot(sums[...], place)
    items = [
        (placed[16 * u : 16 * (u + 1), :128], placed[16 * u : 16 * (u + 1), 128:])
        for u in range(16)
    ]
    for b, (lo, hi) in enumerate(exchange_chunks(items, 1)):
        out[b, 0, :, :128] = lo.astype(BF16)
        out[b, 0, :, 128:] = hi.astype(BF16)


def rows_kernel(
    rows_per_step, band, row_latitude, points, cutoffs, received, waves, table, outer_cos,
    outer_sin, factor, grid_field, out, fourier, twisted, samples
):
    step = pl.program_id(0)

    @pl.when(step == 0)
    def _():
        for g in range(GROUPS):
            items = []
            for src in range(NB):
                block = received[src, g].astype(F32)
                items.append((block[:, :128], block[:, 128:]))
            for row, (lo, hi) in enumerate(exchange_chunks(items, 16)):
                fourier[row, :, 256 * g : 256 * g + 128] = lo
                fourier[row, :, 256 * g + 128 : 256 * g + 256] = hi

    wave = waves[...]
    imag = (lax.broadcasted_iota(jnp.int32, (1, WAVES), 1) & 1) == 1
    sign = jnp.where(imag, F32(-1.0), F32(1.0))
    lane = lax.broadcasted_iota(jnp.int32, (1, 256), 1)
    for r in range(rows_per_step):
        row = step * rows_per_step + r
        lat = row_latitude[band[0] * NB + row] & (points.shape[0] - 1)
        count = points[lat]
        kept = (wave <= cutoffs[lat].astype(F32)).astype(F32)
        weight = kept * jnp.where(wave == 0.0, F32(1.0), F32(2.0))
        x = fourier[row]
        crossed = swap_parts(x) * -weight
        x = x * (weight * sign)
        for b in range(11):
            value = x * outer_cos[r, b : b + 1, :] + crossed * outer_sin[r, b : b + 1, :]
            twisted[r, 16 * b : 16 * (b + 1), :] = value.astype(BF16)
        field = dot(twisted[r], table[r], NT)
        for b in range(11):
            value = jnp.where(lane + 256 * b < count, field[16 * b : 16 * (b + 1), :], 0.0)
            value = value.astype(BF16)
            if b < 10:
                grid_field[r, :, 256 * b : 256 * (b + 1)] = value
                scaled = value.astype(F32) * factor[r, :, 256 * b : 256 * (b + 1)]
                samples[r, 16 * b : 16 * (b + 1), :] = scaled.astype(BF16)
            else:
                value = value[:, :128]
                grid_field[r, :, 2560:2688] = value
                scaled = value.astype(F32) * factor[r, :, 2560:2688]
                samples[r, 160:176, :128] = scaled.astype(BF16)
                samples[r, 160:176, 128:] = jnp.zeros((16, 128), BF16)
        scale = kept / jnp.full((1, WAVES), count.astype(F32))
        for t in range(5):
            lanes = slice(256 * t, 256 * (t + 1))
            part = dot(samples[r], table[r, :, lanes])
            total_cos = jnp.zeros((16, 256), F32)
            total_sin = jnp.zeros((16, 256), F32)
            for b in range(11):
                block = part[16 * b : 16 * (b + 1), :]
                total_cos = total_cos + block * outer_cos[r, b : b + 1, lanes]
                total_sin = total_sin + block * outer_sin[r, b : b + 1, lanes]
            value = sign[:, lanes] * total_cos - swap_parts(total_sin)
            fourier[row, :, lanes] = value * scale[:, lanes]

    @pl.when(step == pl.num_programs(0) - 1)
    def _():
        for g in range(GROUPS):
            items = [
                (fourier[row, :, 256 * g : 256 * g + 128],
                 fourier[row, :, 256 * g + 128 : 256 * g + 256])
                for row in range(NB)
            ]
            for b, (lo, hi) in enumerate(exchange_chunks(items, 16)):
                out[b, g, :, :128] = lo.astype(BF16)
                out[b, g, :, 128:] = hi.astype(BF16)


def mix_kernel(vertical, received, out):
    matrix = vertical[...]
    devices, chunks = received.shape[:2]
    for chunk in range(chunks):
        for g in range(GROUPS):
            block = received[:, chunk, g].reshape(devices * 16, 256)
            value = dot(matrix, block).astype(BF16)
            out[:, chunk, g] = value.reshape(devices, 16, 256)


def final_kernel(truncation, band, slot_pair, lane_latitude, weights, received, legendre, out, sums):
    group = pl.program_id(0)
    width = legendre.shape[1]
    items = []
    for src in range(NB):
        block = received[src, 0].astype(F32)
        items.append((block[:, :128], block[:, 128:]))
    for u, (lo, hi) in enumerate(exchange_chunks(items, 1)):
        sums[16 * u : 16 * (u + 1), :128] = lo.astype(BF16)
        sums[16 * u : 16 * (u + 1), 128:] = hi.astype(BF16)
    target = lax.broadcasted_iota(jnp.int32, (256, 256), 0)
    source = lane_latitude[...]
    value = jnp.where((target >= 128) & (source >= 128), F32(-1.0), F32(1.0))
    fold = jnp.where((target & 127) == (source & 127), value, 0.0).astype(BF16)
    parts = (dot(sums[...], fold, NT) * weights[...]).astype(BF16)
    for s in range(4):
        first, odd = slot_columns(slot_pair[band[0] * 20 + group * 4 + s], width, truncation)
        own = parts[64 * s : 64 * (s + 1)]
        left = jnp.concatenate([own[:, :128], own[:, 128:]], 0)
        full = dot(left, legendre[s], NT)
        even_part = jnp.where(first, full[0:32], full[32:64])
        odd_part = jnp.where(first, full[64:96], full[96:128])
        chosen = jnp.where(odd == 0, even_part, odd_part)
        out[s, 0] = chosen[:16]
        out[s, 1] = chosen[16:]


def whole(shape):
    return pl.BlockSpec(shape, lambda i: (0,) * len(shape))


SMEM = pl.BlockSpec(memory_space=pltpu.SMEM)


def cost(flops, size):
    return pl.CostEstimate(flops=flops, bytes_accessed=size, transcendentals=0)


def per_device(
    spectral, legendre, weights, vertical, grid_factor, points, cutoffs, row_latitude, slot_pair
):
    band = lax.axis_index("band").astype(jnp.int32).reshape(1)
    lev_count = lax.axis_size("lev")
    truncation = 2 * slot_pair.shape[0] - 1
    width = spectral.shape[3]
    row_width = grid_factor.shape[1]
    by_slot = spectral.transpose(2, 1, 0, 3)
    legendre = legendre.transpose(0, 2, 1)
    lane_latitude = row_latitude.reshape(NB, NB).T.reshape(1, 256)
    pairs = slot_pair.reshape(NB, GROUPS, 4).transpose(1, 0, 2)
    waves = jnp.stack([pairs, truncation - pairs], -1)
    waves = jnp.broadcast_to(waves[..., None], waves.shape + (2,)).reshape(1, WAVES).astype(F32)

    message = pl.pallas_call(
        lambda *refs: send_kernel(truncation, *refs),
        grid=(GROUPS,),
        in_specs=[
            SMEM, SMEM, whole((1, 256)),
            pl.BlockSpec((4, 2, 16, width), lambda i: (i, 0, 0, 0)),
            pl.BlockSpec((4, width, 128), lambda i: (i, 0, 0)),
        ],
        out_specs=pl.BlockSpec((NB, 1, 16, 256), lambda i: (0, i, 0, 0)),
        out_shape=jax.ShapeDtypeStruct((NB, GROUPS, 16, 256), BF16),
        scratch_shapes=[pltpu.VMEM((256, 256), BF16)],
        compiler_params=params(),
        cost_estimate=cost(2 * 20 * 128 * 768 * 128, 5_000_000),
        name="legendre_send",
    )(band, slot_pair, lane_latitude, by_slot, legendre)
    received = lax.all_to_all(message, "band", split_axis=0, concat_axis=0, tiled=True)

    per_step = 2
    table, outer_cos, outer_sin = pl.pallas_call(
        lambda *refs: table_kernel(per_step, *refs),
        grid=(NB // per_step,),
        in_specs=[SMEM, SMEM, SMEM, whole((1, WAVES))],
        out_specs=[
            pl.BlockSpec((per_step, 256, WAVES), lambda i: (i, 0, 0)),
            pl.BlockSpec((per_step, 16, WAVES), lambda i: (i, 0, 0)),
            pl.BlockSpec((per_step, 16, WAVES), lambda i: (i, 0, 0)),
        ],
        out_shape=[
            jax.ShapeDtypeStruct((NB, 256, WAVES), BF16),
            jax.ShapeDtypeStruct((NB, 16, WAVES), F32),
            jax.ShapeDtypeStruct((NB, 16, WAVES), F32),
        ],
        scratch_shapes=[pltpu.VMEM((4, 16, WAVES), F32)],
        compiler_params=params(),
        cost_estimate=cost(16 * 256 * 1280 * 20, 14_000_000),
        name="phase_tables",
    )(band, row_latitude, points, waves)

    factor = grid_factor.astype(F32).reshape(NB, 1, row_width)
    grid_field, harmonic = pl.pallas_call(
        lambda *refs: rows_kernel(per_step, *refs),
        grid=(NB // per_step,),
        in_specs=[
            SMEM, SMEM, SMEM, SMEM,
            whole((NB, GROUPS, 16, 256)),
            whole((1, WAVES)),
            pl.BlockSpec((per_step, 256, WAVES), lambda i: (i, 0, 0)),
            pl.BlockSpec((per_step, 16, WAVES), lambda i: (i, 0, 0)),
            pl.BlockSpec((per_step, 16, WAVES), lambda i: (i, 0, 0)),
            pl.BlockSpec((per_step, 1, row_width), lambda i: (i, 0, 0)),
        ],
        out_specs=[
            pl.BlockSpec((per_step, 16, row_width), lambda i: (i, 0, 0)),
            whole((NB, GROUPS, 16, 256)),
        ],
        out_shape=[
            jax.ShapeDtypeStruct((NB, 16, row_width), BF16),
            jax.ShapeDtypeStruct((NB, GROUPS, 16, 256), BF16),
        ],
        scratch_shapes=[
            pltpu.VMEM((NB, 16, WAVES), F32),
            pltpu.VMEM((per_step, 176, WAVES), BF16),
            pltpu.VMEM((per_step, 176, 256), BF16),
        ],
        compiler_params=params(),
        cost_estimate=cost(4 * 16 * 176 * 1280 * 256, 17_000_000),
        name="grid_rows",
    )(band, row_latitude, points, cutoffs, received, waves, table, outer_cos, outer_sin, factor)

    levels_in = lax.all_to_all(harmonic, "lev", split_axis=0, concat_axis=0, tiled=True)
    shape = (lev_count, NB // lev_count, GROUPS, 16, 256)
    mixed = pl.pallas_call(
        mix_kernel,
        grid=(1,),
        in_specs=[whole(vertical.shape), whole(shape)],
        out_specs=whole(shape),
        out_shape=jax.ShapeDtypeStruct(shape, BF16),
        compiler_params=params(),
        cost_estimate=cost(2 * 256 * 256 * 1280, 1_400_000),
        name="vertical_mix",
    )(vertical, levels_in.reshape(shape))
    outgoing = lax.all_to_all(
        mixed.reshape(NB, GROUPS, 16, 256), "lev", split_axis=0, concat_axis=0, tiled=True
    )
    returned = lax.all_to_all(outgoing, "band", split_axis=0, concat_axis=0, tiled=True)

    round_trip = pl.pallas_call(
        lambda *refs: final_kernel(truncation, *refs),
        grid=(GROUPS,),
        in_specs=[
            SMEM, SMEM, whole((1, 256)), whole((1, 256)),
            pl.BlockSpec((NB, 1, 16, 256), lambda i: (0, i, 0, 0)),
            pl.BlockSpec((4, width, 128), lambda i: (i, 0, 0)),
        ],
        out_specs=pl.BlockSpec((4, 2, 16, width), lambda i: (i, 0, 0, 0)),
        out_shape=jax.ShapeDtypeStruct((20, 2, 16, width), F32),
        scratch_shapes=[pltpu.VMEM((256, 256), BF16)],
        compiler_params=params(),
        cost_estimate=cost(2 * 20 * 128 * 768 * 128, 6_000_000),
        name="legendre_return",
    )(
        band, slot_pair, lane_latitude, jnp.concatenate([weights, weights]).reshape(1, 256),
        returned, legendre,
    )
    return (grid_field, round_trip.transpose(2, 1, 0, 3))


def solution(mesh):
    in_specs = (
        P("lev", None, "band", None),
        P("band", None, None),
        P(),
        P(),
        P("band", None),
        P(),
        P(),
        P(),
        P(),
    )
    out_specs = (P("band", "lev", None), P("lev", None, "band", None))
    return jax.shard_map(
        per_device, mesh=mesh, in_specs=in_specs, out_specs=out_specs, check_vma=False
    )
```

```python
import math

import jax
import jax.numpy as jnp
from jax import lax
from jax.experimental import pallas as pl
from jax.experimental.pallas import tpu as pltpu
from jax.sharding import PartitionSpec as P

F32, BF16 = jnp.float32, jnp.bfloat16
NB = 16
GROUPS = 5
WAVES = 1280
ROWS = 2560
COS = (1.0, -19.739208221435547, 64.93938446044922, -85.45658111572266,
       60.241241455078125, -26.39919662475586, 7.783571243286133, -1.4335278272628784)
SIN = (6.2831854820251465, -41.34170150756836, 81.6052474975586, -76.70577239990234,
       42.05741882324219, -15.084507942199707, 3.775092124938965, -0.6134149432182312)
NT = (((1,), (1,)), ((), ()))
FINE, COARSE = 64, 42


def params(limit=24):
    return pltpu.CompilerParams(vmem_limit_bytes=limit * 1024 * 1024)


def dot(a, b, dims=(((1,), (0,)), ((), ()))):
    return lax.dot_general(a, b, dims, preferred_element_type=F32)


def identity():
    same = lax.broadcasted_iota(jnp.int32, (256, 256), 0) == lax.broadcasted_iota(
        jnp.int32, (256, 256), 1
    )
    return same.astype(F32).astype(BF16)


def exchange_chunks(items):
    items = list(items)
    lane = lax.broadcasted_iota(jnp.int32, items[0].shape, 1)
    for level in range(4):
        step = 1 << level
        keep = (lane & step) == 0
        for low in range(16):
            if low & step:
                continue
            a, b = items[low], items[low + step]
            items[low] = jnp.where(keep, a, pltpu.roll(b, step, 1))
            items[low + step] = jnp.where(keep, pltpu.roll(a, 128 - step, 1), b)
    return items


def slot_columns(pair, width, truncation):
    column = lax.broadcasted_iota(jnp.int32, (1, width), 1)
    split = truncation + 1 - pair
    first = column < split
    odd = jnp.where(first, column, column - split) & 1
    return first, odd


def table_kernel(own, row_latitude, points, waves, table, fine, coarse):
    lat = row_latitude[own[0]] & (points.shape[0] - 1)
    for t in range(10):
        lanes = slice(128 * t, 128 * (t + 1))
        wave = waves[:, lanes]
        count = jnp.full((1, 128), points[lat].astype(F32))
        inverse = 1.0 / count

        def circle(rows, stride):
            index = lax.broadcasted_iota(jnp.int32, (rows, 128), 0).astype(F32)
            product = (wave * stride) * index
            turns = jnp.floor(product * inverse + 0.5)
            y = (product - turns * count) * inverse
            z = y * y
            c = jnp.full_like(z, COS[-1])
            s = jnp.full_like(z, SIN[-1])
            for k in range(6, -1, -1):
                c = c * z + COS[k]
                s = s * z + SIN[k]
            return c, s * y

        imag = (lax.broadcasted_iota(jnp.int32, (1, 128), 1) & 16) == 16
        fine[0], fine[1] = circle(FINE, 1.0)
        c2, s2 = circle(48, float(FINE))
        coarse[0] = jnp.where(imag, s2, c2)
        coarse[1] = jnp.where(imag, -c2, s2)
        for a in range(COARSE):
            value = coarse[0, a : a + 1, :] * fine[0] - coarse[1, a : a + 1, :] * fine[1]
            table[FINE * a : FINE * (a + 1), lanes] = value.astype(BF16)


def send_kernel(truncation, band, slot_pair, lane_latitude, spectral, legendre, out, sums, place, rows):
    group = pl.program_id(0)
    width = spectral.shape[-1]

    @pl.when(group == 0)
    def _():
        hit = lax.broadcasted_iota(jnp.int32, (256, 256), 0) == lane_latitude[...]
        place[...] = dot(identity(), hit.astype(F32).astype(BF16), NT).astype(BF16)

    for s in range(4):
        first, odd = slot_columns(slot_pair[band[0] * 20 + group * 4 + s], width, truncation)
        one = first.astype(F32)
        sign = 1.0 - 2.0 * odd.astype(F32)
        x = spectral[s].reshape(32, width)
        picks = [one, 1.0 - one, one * sign, (1.0 - one) * sign]
        left = jnp.concatenate([x * p.astype(BF16) for p in picks], 0)
        values = dot(left, legendre[s]).astype(BF16)
        sums[64 * s : 64 * (s + 1), :128] = values[:64]
        sums[64 * s : 64 * (s + 1), 128:] = values[64:]
    placed = dot(place[...], sums[...], NT)
    rows[pl.ds(2 * group, 256, stride=10), :] = placed[:, :128]
    rows[pl.ds(2 * group + 1, 256, stride=10), :] = placed[:, 128:]

    @pl.when(group == GROUPS - 1)
    def _():
        out[...] = rows[...].astype(BF16)


def row_kernel(
    own, row_latitude, points, cutoffs, received, waves, table, vertical, factor, grid_field, out,
    rows, fourier, left, samples
):
    lat = row_latitude[own[0]] & (points.shape[0] - 1)
    count = points[lat]
    wave = waves[...]
    imag = (lax.broadcasted_iota(jnp.int32, (1, WAVES), 1) & 16) == 16
    sign = jnp.where(imag, F32(-1.0), F32(1.0))
    kept = sign * (wave <= cutoffs[lat].astype(F32)).astype(F32)
    weight = kept * jnp.where(wave == 0.0, F32(1.0), F32(2.0))
    scale = kept / jnp.full((1, WAVES), count.astype(F32))
    rows[...] = received[...].astype(F32)
    for c in range(10):
        items = [rows[pl.ds(160 * b + c, 16, stride=10), :] for b in range(16)]
        lanes = slice(128 * c, 128 * (c + 1))
        for l, item in enumerate(exchange_chunks(items)):
            fourier[pl.ds(256 * c + l, 16, stride=16), :] = item * weight[:, lanes]
        left[:, lanes] = fourier[256 * c : 256 * (c + 1), :].astype(BF16)
    lane = lax.broadcasted_iota(jnp.int32, (1, 256), 1)
    width = grid_field.shape[1]
    for start in range(0, width, 256):
        size = min(256, width - start)
        cut = slice(start, start + size)
        field = dot(left[...], table[cut, :], NT)
        field = jnp.where(lane[:, :size] + start < count, field, 0.0).astype(BF16)
        grid_field[:, cut] = field
        samples[:, cut] = (dot(vertical[...], field) * factor[:, cut]).astype(BF16)
    for t in range(5):
        lanes = slice(256 * t, 256 * (t + 1))
        value = dot(samples[...], table[:, lanes]) * scale[:, lanes]
        fourier[512 * t : 512 * t + 256, :] = value[:, :128]
        fourier[512 * t + 256 : 512 * (t + 1), :] = value[:, 128:]
    for c in range(10):
        items = [fourier[pl.ds(256 * c + l, 16, stride=16), :] for l in range(16)]
        for b, item in enumerate(exchange_chunks(items)):
            rows[pl.ds(160 * b + c, 16, stride=10), :] = item
    out[...] = rows[...].astype(BF16)


def final_kernel(truncation, band, slot_pair, lane_latitude, weights, received, legendre, out, rows):
    group = pl.program_id(0)
    width = legendre.shape[1]

    @pl.when(group == 0)
    def _():
        rows[...] = received[...].astype(F32)

    values = jnp.concatenate(
        [rows[pl.ds(2 * group + h, 256, stride=10), :].astype(BF16) for h in (0, 1)], 1
    )
    turned = dot(identity(), values, NT).astype(BF16)
    target = lax.broadcasted_iota(jnp.int32, (256, 256), 0)
    source = lane_latitude[...]
    value = jnp.where((target >= 128) & (source >= 128), F32(-1.0), F32(1.0))
    fold = jnp.where((target & 127) == (source & 127), value, 0.0).astype(BF16)
    parts = (dot(turned, fold, NT) * weights[...]).astype(BF16)
    for s in range(4):
        first, odd = slot_columns(slot_pair[band[0] * 20 + group * 4 + s], width, truncation)
        own = parts[64 * s : 64 * (s + 1)]
        left = jnp.concatenate([own[:, :128], own[:, 128:]], 0)
        full = dot(left, legendre[s], NT)
        even_part = jnp.where(first, full[0:32], full[32:64])
        odd_part = jnp.where(first, full[64:96], full[96:128])
        chosen = jnp.where(odd == 0, even_part, odd_part)
        out[s, 0] = chosen[:16]
        out[s, 1] = chosen[16:]


def whole(shape):
    return pl.BlockSpec(shape, lambda i: (0,) * len(shape))


SMEM = pl.BlockSpec(memory_space=pltpu.SMEM)
VMEM = pl.BlockSpec(memory_space=pltpu.VMEM)


def cost(flops, size):
    return pl.CostEstimate(flops=flops, bytes_accessed=size, transcendentals=0)


def everywhere(message):
    pieces = message.reshape(ROWS // 2, 2, 128)
    pieces = lax.all_to_all(pieces, ("band", "lev"), split_axis=0, concat_axis=0, tiled=True)
    return pieces.reshape(ROWS, 128)


def per_device(
    spectral, legendre, weights, vertical, grid_factor, points, cutoffs, row_latitude, slot_pair
):
    band_index = lax.axis_index("band").astype(jnp.int32)
    lev_index = lax.axis_index("lev").astype(jnp.int32)
    band = band_index.reshape(1)
    own = (band_index * NB + lev_index).reshape(1)
    truncation = 2 * slot_pair.shape[0] - 1
    width = spectral.shape[3]
    row_width = grid_factor.shape[1]
    by_slot = spectral.transpose(2, 1, 0, 3)
    legendre = legendre.transpose(0, 2, 1)
    lane_latitude = row_latitude.reshape(1, 256)
    pairs = slot_pair.reshape(NB, GROUPS, 4).transpose(1, 2, 0)
    waves = jnp.stack([pairs, pairs, truncation - pairs, truncation - pairs], 2)
    waves = waves.reshape(1, WAVES).astype(F32)
    factor = lax.dynamic_slice_in_dim(grid_factor, lev_index, 1, 0).astype(F32)

    message = pl.pallas_call(
        lambda *refs: send_kernel(truncation, *refs),
        grid=(GROUPS,),
        in_specs=[
            SMEM, SMEM, whole((1, 256)),
            pl.BlockSpec((4, 2, 16, width), lambda i: (i, 0, 0, 0)),
            pl.BlockSpec((4, width, 128), lambda i: (i, 0, 0)),
        ],
        out_specs=whole((ROWS, 128)),
        out_shape=jax.ShapeDtypeStruct((ROWS, 128), BF16),
        scratch_shapes=[
            pltpu.VMEM((256, 256), BF16),
            pltpu.VMEM((256, 256), BF16),
            pltpu.VMEM((ROWS, 128), F32),
        ],
        compiler_params=params(),
        cost_estimate=cost(2 * 20 * 128 * 768 * 128, 5_000_000),
        name="legendre_send",
    )(band, slot_pair, lane_latitude, by_slot, legendre)
    received = everywhere(message)

    table = pl.pallas_call(
        table_kernel,
        in_specs=[SMEM, SMEM, SMEM, VMEM],
        out_specs=VMEM,
        out_shape=jax.ShapeDtypeStruct((row_width, WAVES), BF16),
        scratch_shapes=[pltpu.VMEM((2, FINE, 128), F32), pltpu.VMEM((2, 48, 128), F32)],
        compiler_params=params(),
        cost_estimate=cost(2688 * 1280 * 10, 7_000_000),
        name="phase_table",
    )(own, row_latitude, points, waves)

    grid_row, outgoing = pl.pallas_call(
        row_kernel,
        in_specs=[SMEM, SMEM, SMEM, SMEM, VMEM, VMEM, VMEM, VMEM, VMEM],
        out_specs=[VMEM, VMEM],
        out_shape=[
            jax.ShapeDtypeStruct((256, row_width), BF16),
            jax.ShapeDtypeStruct((ROWS, 128), BF16),
        ],
        scratch_shapes=[
            pltpu.VMEM((ROWS, 128), F32),
            pltpu.VMEM((ROWS, 128), F32),
            pltpu.VMEM((256, WAVES), BF16),
            pltpu.VMEM((256, row_width), BF16),
        ],
        compiler_params=params(),
        cost_estimate=cost(4 * 256 * 2688 * 1280, 10_000_000),
        name="grid_row",
    )(own, row_latitude, points, cutoffs, received, waves, table, vertical, factor)

    returned = everywhere(outgoing)
    grid_row, returned = lax.optimization_barrier((grid_row, returned))
    grid_field = lax.all_to_all(
        grid_row.reshape(NB, NB, row_width), "lev", split_axis=0, concat_axis=0, tiled=True
    )

    round_trip = pl.pallas_call(
        lambda *refs: final_kernel(truncation, *refs),
        grid=(GROUPS,),
        in_specs=[
            SMEM, SMEM, whole((1, 256)), whole((1, 256)), whole((ROWS, 128)),
            pl.BlockSpec((4, width, 128), lambda i: (i, 0, 0)),
        ],
        out_specs=pl.BlockSpec((4, 2, 16, width), lambda i: (i, 0, 0, 0)),
        out_shape=jax.ShapeDtypeStruct((20, 2, 16, width), F32),
        scratch_shapes=[pltpu.VMEM((ROWS, 128), F32)],
        compiler_params=params(),
        cost_estimate=cost(2 * 20 * 128 * 768 * 128, 6_000_000),
        name="legendre_return",
    )(
        band, slot_pair, lane_latitude, jnp.concatenate([weights, weights]).reshape(1, 256),
        returned, legendre,
    )
    return (grid_field, round_trip.transpose(2, 1, 0, 3))


def solution(mesh):
    in_specs = (
        P("lev", None, "band", None),
        P("band", None, None),
        P(),
        P(),
        P("band", None),
        P(),
        P(),
        P(),
        P(),
    )
    out_specs = (P("band", "lev", None), P("lev", None, "band", None))
    return jax.shard_map(
        per_device, mesh=mesh, in_specs=in_specs, out_specs=out_specs, check_vma=False
    )
```

```python
import math

import jax
import jax.numpy as jnp
from jax import lax
from jax.experimental import pallas as pl
from jax.experimental.pallas import tpu as pltpu
from jax.sharding import PartitionSpec as P

F32, BF16 = jnp.float32, jnp.bfloat16
NB = 16
GROUPS = 5
ROWS = 2560
WAVES = 1280
COS = (1.0, -19.739208221435547, 64.93938446044922, -85.45658111572266,
       60.241241455078125, -26.39919662475586, 7.783571243286133, -1.4335278272628784)
SIN = (6.2831854820251465, -41.34170150756836, 81.6052474975586, -76.70577239990234,
       42.05741882324219, -15.084507942199707, 3.775092124938965, -0.6134149432182312)
NT = (((1,), (1,)), ((), ()))


def params(limit=24):
    return pltpu.CompilerParams(vmem_limit_bytes=limit * 1024 * 1024)


def dot(a, b, dims=(((1,), (0,)), ((), ()))):
    return lax.dot_general(a, b, dims, preferred_element_type=F32)


def exchange_chunks(items, width):
    items = list(items)
    lane = lax.broadcasted_iota(jnp.int32, items[0][0].shape, 1)
    for level in range(4):
        step = 1 << level
        shift = width * step
        for low in range(16):
            if low & step:
                continue
            a, b = items[low], items[low + step]
            if shift == 128:
                items[low], items[low + step] = (a[0], b[0]), (a[1], b[1])
                continue
            keep = (lane & shift) == 0
            items[low] = tuple(jnp.where(keep, a[h], pltpu.roll(b[h], shift, 1)) for h in (0, 1))
            items[low + step] = tuple(
                jnp.where(keep, pltpu.roll(a[h], 128 - shift, 1), b[h]) for h in (0, 1)
            )
    return items


def exchange_lanes(items, width):
    items = list(items)
    lane = lax.broadcasted_iota(jnp.int32, items[0].shape, 1)
    count = len(items)
    for level in range(count.bit_length() - 1):
        step = 1 << level
        shift = width * step
        keep = (lane & shift) == 0
        for low in range(count):
            if low & step:
                continue
            a, b = items[low], items[low + step]
            items[low] = jnp.where(keep, a, pltpu.roll(b, shift, 1))
            items[low + step] = jnp.where(keep, pltpu.roll(a, 128 - shift, 1), b)
    return items


def swap_parts(x):
    lane = lax.broadcasted_iota(jnp.int32, (x.shape[0], 128), 1)
    even = (lane & 1) == 0
    pieces = []
    for t in range(x.shape[1] // 128):
        piece = x[:, 128 * t : 128 * (t + 1)]
        pieces.append(jnp.where(even, pltpu.roll(piece, 127, 1), pltpu.roll(piece, 1, 1)))
    return jnp.concatenate(pieces, 1)


def slot_columns(pair, width, truncation):
    column = lax.broadcasted_iota(jnp.int32, (1, width), 1)
    split = truncation + 1 - pair
    first = column < split
    odd = jnp.where(first, column, column - split) & 1
    return first, odd


def table_kernel(rows_per_step, band, row_latitude, points, waves, table, outer_cos, outer_sin, seeds):
    step = pl.program_id(0)
    wave = waves[...]
    imag = (lax.broadcasted_iota(jnp.int32, (1, WAVES), 1) & 1) == 1
    index = lax.broadcasted_iota(jnp.int32, (16, WAVES), 0).astype(F32)
    for r in range(rows_per_step):
        lat = row_latitude[band[0] * NB + step * rows_per_step + r] & (points.shape[0] - 1)
        count = jnp.full((1, WAVES), points[lat].astype(F32))
        inverse = 1.0 / count

        def circle(stride):
            product = (wave * stride) * index
            turns = jnp.floor(product * inverse + 0.5)
            y = (product - turns * count) * inverse
            z = y * y
            c = jnp.full_like(z, COS[-1])
            s = jnp.full_like(z, SIN[-1])
            for k in range(6, -1, -1):
                c = c * z + COS[k]
                s = s * z + SIN[k]
            return c, s * y

        c1, s1 = circle(1.0)
        c2, s2 = circle(16.0)
        seeds[0] = jnp.where(imag, s2, c2)
        seeds[1] = jnp.where(imag, -c2, s2)
        seeds[2] = c1
        seeds[3] = s1
        c3, s3 = circle(256.0)
        outer_cos[r] = c3
        outer_sin[r] = s3
        for t in range(5):
            lanes = slice(256 * t, 256 * (t + 1))
            c1, s1 = seeds[2, :, lanes], seeds[3, :, lanes]
            for a in range(16):
                value = seeds[0, a : a + 1, lanes] * c1 - seeds[1, a : a + 1, lanes] * s1
                table[r, 16 * a : 16 * (a + 1), lanes] = value.astype(BF16)


def send_kernel(truncation, band, slot_pair, lane_latitude, spectral, legendre, out, sums):
    group = pl.program_id(0)
    width = spectral.shape[-1]
    place = (
        lax.broadcasted_iota(jnp.int32, (256, 256), 0) == lane_latitude[...]
    ).astype(F32).astype(BF16)
    for s in range(4):
        first, odd = slot_columns(slot_pair[band[0] * 20 + group * 4 + s], width, truncation)
        one = first.astype(F32)
        sign = 1.0 - 2.0 * odd.astype(F32)
        x = spectral[s].reshape(32, width)
        picks = [one, 1.0 - one, one * sign, (1.0 - one) * sign]
        left = jnp.concatenate([x * p.astype(BF16) for p in picks], 0)
        values = dot(left, legendre[s]).astype(BF16)
        sums[64 * s : 64 * (s + 1), :128] = values[:64]
        sums[64 * s : 64 * (s + 1), 128:] = values[64:]
    placed = dot(sums[...], place)
    items = [
        (placed[16 * u : 16 * (u + 1), :128], placed[16 * u : 16 * (u + 1), 128:])
        for u in range(16)
    ]
    for b, (lo, hi) in enumerate(exchange_chunks(items, 1)):
        out[b, 0, :, :128] = lo.astype(BF16)
        out[b, 0, :, 128:] = hi.astype(BF16)


def rows_kernel(
    rows_per_step, band, row_latitude, points, cutoffs, received, waves, table, outer_cos,
    outer_sin, factor, grid_field, out, fourier, twisted, samples
):
    step = pl.program_id(0)

    @pl.when(step == 0)
    def _():
        for g in range(GROUPS):
            items = []
            for src in range(NB):
                block = received[src, g].astype(F32)
                items.append((block[:, :128], block[:, 128:]))
            for row, (lo, hi) in enumerate(exchange_chunks(items, 16)):
                fourier[row, :, 256 * g : 256 * g + 128] = lo
                fourier[row, :, 256 * g + 128 : 256 * g + 256] = hi

    wave = waves[...]
    imag = (lax.broadcasted_iota(jnp.int32, (1, WAVES), 1) & 1) == 1
    sign = jnp.where(imag, F32(-1.0), F32(1.0))
    lane = lax.broadcasted_iota(jnp.int32, (1, 256), 1)
    for r in range(rows_per_step):
        row = step * rows_per_step + r
        lat = row_latitude[band[0] * NB + row] & (points.shape[0] - 1)
        count = points[lat]
        kept = (wave <= cutoffs[lat].astype(F32)).astype(F32)
        weight = kept * jnp.where(wave == 0.0, F32(1.0), F32(2.0))
        x = fourier[row]
        crossed = swap_parts(x) * -weight
        x = x * (weight * sign)
        for b in range(11):
            value = x * outer_cos[r, b : b + 1, :] + crossed * outer_sin[r, b : b + 1, :]
            twisted[r, 16 * b : 16 * (b + 1), :] = value.astype(BF16)
        field = dot(twisted[r], table[r], NT)
        for b in range(11):
            value = jnp.where(lane + 256 * b < count, field[16 * b : 16 * (b + 1), :], 0.0)
            value = value.astype(BF16)
            if b < 10:
                grid_field[r, :, 256 * b : 256 * (b + 1)] = value
                scaled = value.astype(F32) * factor[r, :, 256 * b : 256 * (b + 1)]
                samples[r, 16 * b : 16 * (b + 1), :] = scaled.astype(BF16)
            else:
                value = value[:, :128]
                grid_field[r, :, 2560:2688] = value
                scaled = value.astype(F32) * factor[r, :, 2560:2688]
                samples[r, 160:176, :128] = scaled.astype(BF16)
                samples[r, 160:176, 128:] = jnp.zeros((16, 128), BF16)
        scale = kept / jnp.full((1, WAVES), count.astype(F32))
        for t in range(5):
            lanes = slice(256 * t, 256 * (t + 1))
            part = dot(samples[r], table[r, :, lanes])
            total_cos = jnp.zeros((16, 256), F32)
            total_sin = jnp.zeros((16, 256), F32)
            for b in range(11):
                block = part[16 * b : 16 * (b + 1), :]
                total_cos = total_cos + block * outer_cos[r, b : b + 1, lanes]
                total_sin = total_sin + block * outer_sin[r, b : b + 1, lanes]
            value = sign[:, lanes] * total_cos - swap_parts(total_sin)
            out[r, :, lanes] = (value * scale[:, lanes]).astype(BF16)


def mix_kernel(vertical, received, out, levels, rows):
    block = received[...].reshape(256, WAVES)
    for t in range(10):
        levels[256 * t : 256 * (t + 1), :] = dot(vertical[...], block[:, 128 * t : 128 * (t + 1)])
    for t in range(10):
        for high in range(2):
            first = 256 * t + 8 * high
            items = [levels[pl.ds(first + l, 16, stride=16), :] for l in range(8)]
            for b, item in enumerate(exchange_lanes(items, 16)):
                start = 160 * (8 * (t % 2) + b) + 2 * (t // 2) + high
                rows[pl.ds(start, 16, stride=10), :] = item
    out[...] = rows[...].astype(BF16)


def final_kernel(truncation, band, slot_pair, lane_latitude, weights, received, legendre, out, rows):
    group = pl.program_id(0)
    width = legendre.shape[1]

    @pl.when(group == 0)
    def _():
        rows[...] = received[...].astype(F32)

    values = jnp.concatenate(
        [rows[pl.ds(2 * group + h, 256, stride=10), :].astype(BF16) for h in (0, 1)], 1
    )
    target = lax.broadcasted_iota(jnp.int32, (256, 256), 0)
    lane = lax.broadcasted_iota(jnp.int32, (256, 256), 1)
    swap = (lane >> 4 == (target & 15)) & ((lane & 15) == target >> 4)
    turned = dot(swap.astype(F32).astype(BF16), values, NT).astype(BF16)
    source = lane_latitude[...]
    value = jnp.where((target >= 128) & (source >= 128), F32(-1.0), F32(1.0))
    fold = jnp.where((target & 127) == (source & 127), value, 0.0).astype(BF16)
    parts = (dot(turned, fold, NT) * weights[...]).astype(BF16)
    for s in range(4):
        first, odd = slot_columns(slot_pair[band[0] * 20 + group * 4 + s], width, truncation)
        own = parts[64 * s : 64 * (s + 1)]
        left = jnp.concatenate([own[:, :128], own[:, 128:]], 0)
        full = dot(left, legendre[s], NT)
        even_part = jnp.where(first, full[0:32], full[32:64])
        odd_part = jnp.where(first, full[64:96], full[96:128])
        chosen = jnp.where(odd == 0, even_part, odd_part)
        out[s, 0] = chosen[:16]
        out[s, 1] = chosen[16:]


def whole(shape):
    return pl.BlockSpec(shape, lambda i: (0,) * len(shape))


SMEM = pl.BlockSpec(memory_space=pltpu.SMEM)
VMEM = pl.BlockSpec(memory_space=pltpu.VMEM)


def cost(flops, size):
    return pl.CostEstimate(flops=flops, bytes_accessed=size, transcendentals=0)


def everywhere(message):
    pieces = message.reshape(ROWS // 2, 2, 128)
    pieces = lax.all_to_all(pieces, ("band", "lev"), split_axis=0, concat_axis=0, tiled=True)
    return pieces.reshape(ROWS, 128)


def per_device(
    spectral, legendre, weights, vertical, grid_factor, points, cutoffs, row_latitude, slot_pair
):
    band = lax.axis_index("band").astype(jnp.int32).reshape(1)
    truncation = 2 * slot_pair.shape[0] - 1
    width = spectral.shape[3]
    row_width = grid_factor.shape[1]
    by_slot = spectral.transpose(2, 1, 0, 3)
    legendre = legendre.transpose(0, 2, 1)
    lane_latitude = row_latitude.reshape(NB, NB).T.reshape(1, 256)
    pairs = slot_pair.reshape(NB, GROUPS, 4).transpose(1, 0, 2)
    waves = jnp.stack([pairs, truncation - pairs], -1)
    waves = jnp.broadcast_to(waves[..., None], waves.shape + (2,)).reshape(1, WAVES).astype(F32)

    message = pl.pallas_call(
        lambda *refs: send_kernel(truncation, *refs),
        grid=(GROUPS,),
        in_specs=[
            SMEM, SMEM, whole((1, 256)),
            pl.BlockSpec((4, 2, 16, width), lambda i: (i, 0, 0, 0)),
            pl.BlockSpec((4, width, 128), lambda i: (i, 0, 0)),
        ],
        out_specs=pl.BlockSpec((NB, 1, 16, 256), lambda i: (0, i, 0, 0)),
        out_shape=jax.ShapeDtypeStruct((NB, GROUPS, 16, 256), BF16),
        scratch_shapes=[pltpu.VMEM((256, 256), BF16)],
        compiler_params=params(),
        cost_estimate=cost(2 * 20 * 128 * 768 * 128, 5_000_000),
        name="legendre_send",
    )(band, slot_pair, lane_latitude, by_slot, legendre)
    received = lax.all_to_all(message, "band", split_axis=0, concat_axis=0, tiled=True)

    per_step = 2
    table, outer_cos, outer_sin = pl.pallas_call(
        lambda *refs: table_kernel(per_step, *refs),
        grid=(NB // per_step,),
        in_specs=[SMEM, SMEM, SMEM, whole((1, WAVES))],
        out_specs=[
            pl.BlockSpec((per_step, 256, WAVES), lambda i: (i, 0, 0)),
            pl.BlockSpec((per_step, 16, WAVES), lambda i: (i, 0, 0)),
            pl.BlockSpec((per_step, 16, WAVES), lambda i: (i, 0, 0)),
        ],
        out_shape=[
            jax.ShapeDtypeStruct((NB, 256, WAVES), BF16),
            jax.ShapeDtypeStruct((NB, 16, WAVES), F32),
            jax.ShapeDtypeStruct((NB, 16, WAVES), F32),
        ],
        scratch_shapes=[pltpu.VMEM((4, 16, WAVES), F32)],
        compiler_params=params(),
        cost_estimate=cost(16 * 256 * 1280 * 20, 14_000_000),
        name="phase_tables",
    )(band, row_latitude, points, waves)

    factor = grid_factor.astype(F32).reshape(NB, 1, row_width)
    grid_field, harmonic = pl.pallas_call(
        lambda *refs: rows_kernel(per_step, *refs),
        grid=(NB // per_step,),
        in_specs=[
            SMEM, SMEM, SMEM, SMEM,
            whole((NB, GROUPS, 16, 256)),
            whole((1, WAVES)),
            pl.BlockSpec((per_step, 256, WAVES), lambda i: (i, 0, 0)),
            pl.BlockSpec((per_step, 16, WAVES), lambda i: (i, 0, 0)),
            pl.BlockSpec((per_step, 16, WAVES), lambda i: (i, 0, 0)),
            pl.BlockSpec((per_step, 1, row_width), lambda i: (i, 0, 0)),
        ],
        out_specs=[
            pl.BlockSpec((per_step, 16, row_width), lambda i: (i, 0, 0)),
            pl.BlockSpec((per_step, 16, WAVES), lambda i: (i, 0, 0)),
        ],
        out_shape=[
            jax.ShapeDtypeStruct((NB, 16, row_width), BF16),
            jax.ShapeDtypeStruct((NB, 16, WAVES), BF16),
        ],
        scratch_shapes=[
            pltpu.VMEM((NB, 16, WAVES), F32),
            pltpu.VMEM((per_step, 176, WAVES), BF16),
            pltpu.VMEM((per_step, 176, 256), BF16),
        ],
        compiler_params=params(),
        cost_estimate=cost(4 * 16 * 176 * 1280 * 256, 17_000_000),
        name="grid_rows",
    )(band, row_latitude, points, cutoffs, received, waves, table, outer_cos, outer_sin, factor)

    levels_in = lax.all_to_all(harmonic, "lev", split_axis=0, concat_axis=0, tiled=True)
    outgoing = pl.pallas_call(
        mix_kernel,
        in_specs=[VMEM, VMEM],
        out_specs=VMEM,
        out_shape=jax.ShapeDtypeStruct((ROWS, 128), BF16),
        scratch_shapes=[pltpu.VMEM((ROWS, 128), F32), pltpu.VMEM((ROWS, 128), F32)],
        compiler_params=params(),
        cost_estimate=cost(2 * 256 * 256 * 1280, 1_400_000),
        name="vertical_mix",
    )(vertical, levels_in)
    returned = everywhere(outgoing)

    round_trip = pl.pallas_call(
        lambda *refs: final_kernel(truncation, *refs),
        grid=(GROUPS,),
        in_specs=[
            SMEM, SMEM, whole((1, 256)), whole((1, 256)), whole((ROWS, 128)),
            pl.BlockSpec((4, width, 128), lambda i: (i, 0, 0)),
        ],
        out_specs=pl.BlockSpec((4, 2, 16, width), lambda i: (i, 0, 0, 0)),
        out_shape=jax.ShapeDtypeStruct((20, 2, 16, width), F32),
        scratch_shapes=[pltpu.VMEM((ROWS, 128), F32)],
        compiler_params=params(),
        cost_estimate=cost(2 * 20 * 128 * 768 * 128, 6_000_000),
        name="legendre_return",
    )(
        band, slot_pair, row_latitude.reshape(1, 256), jnp.concatenate([weights, weights]).reshape(1, 256),
        returned, legendre,
    )
    return (grid_field, round_trip.transpose(2, 1, 0, 3))


def solution(mesh):
    in_specs = (
        P("lev", None, "band", None),
        P("band", None, None),
        P(),
        P(),
        P("band", None),
        P(),
        P(),
        P(),
        P(),
    )
    out_specs = (P("band", "lev", None), P("lev", None, "band", None))
    return jax.shard_map(
        per_device, mesh=mesh, in_specs=in_specs, out_specs=out_specs, check_vma=False
    )
```

```python
import math

import jax
import jax.numpy as jnp
from jax import lax
from jax.experimental import pallas as pl
from jax.experimental.pallas import tpu as pltpu
from jax.sharding import PartitionSpec as P

F32, BF16 = jnp.float32, jnp.bfloat16
NB = 16
GROUPS = 5
ROWS = 2560
WAVES = 1280
COS = (1.0, -19.739208221435547, 64.93938446044922, -85.45658111572266,
       60.241241455078125, -26.39919662475586, 7.783571243286133, -1.4335278272628784)
SIN = (6.2831854820251465, -41.34170150756836, 81.6052474975586, -76.70577239990234,
       42.05741882324219, -15.084507942199707, 3.775092124938965, -0.6134149432182312)
NT = (((1,), (1,)), ((), ()))


def params(limit=24):
    return pltpu.CompilerParams(vmem_limit_bytes=limit * 1024 * 1024)


def dot(a, b, dims=(((1,), (0,)), ((), ()))):
    return lax.dot_general(a, b, dims, preferred_element_type=F32)


def exchange_chunks(items, width):
    items = list(items)
    lane = lax.broadcasted_iota(jnp.int32, items[0][0].shape, 1)
    for level in range(4):
        step = 1 << level
        shift = width * step
        for low in range(16):
            if low & step:
                continue
            a, b = items[low], items[low + step]
            if shift == 128:
                items[low], items[low + step] = (a[0], b[0]), (a[1], b[1])
                continue
            keep = (lane & shift) == 0
            items[low] = tuple(jnp.where(keep, a[h], pltpu.roll(b[h], shift, 1)) for h in (0, 1))
            items[low + step] = tuple(
                jnp.where(keep, pltpu.roll(a[h], 128 - shift, 1), b[h]) for h in (0, 1)
            )
    return items


def exchange_lanes(items, width):
    items = list(items)
    lane = lax.broadcasted_iota(jnp.int32, items[0].shape, 1)
    count = len(items)
    for level in range(count.bit_length() - 1):
        step = 1 << level
        shift = width * step
        keep = (lane & shift) == 0
        for low in range(count):
            if low & step:
                continue
            a, b = items[low], items[low + step]
            items[low] = jnp.where(keep, a, pltpu.roll(b, shift, 1))
            items[low + step] = jnp.where(keep, pltpu.roll(a, 128 - shift, 1), b)
    return items


def swap_parts(x):
    lane = lax.broadcasted_iota(jnp.int32, (x.shape[0], 128), 1)
    even = (lane & 1) == 0
    pieces = []
    for t in range(x.shape[1] // 128):
        piece = x[:, 128 * t : 128 * (t + 1)]
        pieces.append(jnp.where(even, pltpu.roll(piece, 127, 1), pltpu.roll(piece, 1, 1)))
    return jnp.concatenate(pieces, 1)


def slot_columns(pair, width, truncation):
    column = lax.broadcasted_iota(jnp.int32, (1, width), 1)
    split = truncation + 1 - pair
    first = column < split
    odd = jnp.where(first, column, column - split) & 1
    return first, odd


def table_kernel(rows_per_step, band, row_latitude, points, waves, table, outer_cos, outer_sin, seeds):
    step = pl.program_id(0)
    wave = waves[...]
    imag = (lax.broadcasted_iota(jnp.int32, (1, WAVES), 1) & 1) == 1
    index = lax.broadcasted_iota(jnp.int32, (16, WAVES), 0).astype(F32)
    for r in range(rows_per_step):
        lat = row_latitude[band[0] * NB + step * rows_per_step + r] & (points.shape[0] - 1)
        count = jnp.full((1, WAVES), points[lat].astype(F32))
        inverse = 1.0 / count

        def circle(stride):
            product = (wave * stride) * index
            turns = jnp.floor(product * inverse + 0.5)
            y = (product - turns * count) * inverse
            z = y * y
            c = jnp.full_like(z, COS[-1])
            s = jnp.full_like(z, SIN[-1])
            for k in range(6, -1, -1):
                c = c * z + COS[k]
                s = s * z + SIN[k]
            return c, s * y

        c1, s1 = circle(1.0)
        c2, s2 = circle(16.0)
        seeds[0] = jnp.where(imag, s2, c2)
        seeds[1] = jnp.where(imag, -c2, s2)
        seeds[2] = c1
        seeds[3] = s1
        c3, s3 = circle(256.0)
        outer_cos[r] = c3
        outer_sin[r] = s3
        for t in range(5):
            lanes = slice(256 * t, 256 * (t + 1))
            c1, s1 = seeds[2, :, lanes], seeds[3, :, lanes]
            for a in range(16):
                value = seeds[0, a : a + 1, lanes] * c1 - seeds[1, a : a + 1, lanes] * s1
                table[r, 16 * a : 16 * (a + 1), lanes] = value.astype(BF16)


def send_kernel(
    truncation, band, slot_pair, lane_latitude, spectral, legendre, out, sums, spread, spectral_in,
    legendre_in, messages, ready, sent
):
    width = spectral.shape[-1]
    whole_spectral = pltpu.make_async_copy(spectral, spectral_in, ready.at[GROUPS])
    whole_spectral.start()
    copies = []
    for g in range(GROUPS):
        cut = pl.ds(4 * g, 4)
        copies.append(pltpu.make_async_copy(legendre.at[cut], legendre_in.at[cut], ready.at[g]))
        copies[g].start()
    place = (
        lax.broadcasted_iota(jnp.int32, (256, 256), 0) == lane_latitude[...]
    ).astype(F32).astype(BF16)
    whole_spectral.wait()
    for g in range(GROUPS):
        copies[g].wait()
        values = []
        for s in range(4 * g, 4 * g + 4):
            first, odd = slot_columns(slot_pair[band[0] * 20 + s], width, truncation)
            one = first.astype(F32)
            sign = 1.0 - 2.0 * odd.astype(F32)
            x = spectral_in[:, s].reshape(32, width)
            picks = [one, 1.0 - one, one * sign, (1.0 - one) * sign]
            left = jnp.concatenate([x * p.astype(BF16) for p in picks], 0)
            values.append(dot(left, legendre_in[s]).astype(BF16))
        for s in range(4):
            sums[g, 64 * s : 64 * (s + 1), :128] = values[s][:64]
            sums[g, 64 * s : 64 * (s + 1), 128:] = values[s][64:]
    for g in range(GROUPS):
        placed = dot(sums[g], place)
        spread[g, 0] = placed[:, :128]
        spread[g, 1] = placed[:, 128:]
        items = []
        for u in range(16):
            at = pl.ds(32 * (u >> 1) + (u & 1), 16, stride=2)
            items.append((spread[g, 0, at, :], spread[g, 1, at, :]))
        for b, (lo, hi) in enumerate(exchange_chunks(items, 1)):
            messages[b, g, :, :128] = lo.astype(BF16)
            messages[b, g, :, 128:] = hi.astype(BF16)
        cut = pl.ds(g, 1)
        copies[g] = pltpu.make_async_copy(messages.at[:, cut], out.at[:, cut], sent.at[g])
        copies[g].start()
    for copy in copies:
        copy.wait()


def rows_kernel(
    rows_per_step, band, row_latitude, points, cutoffs, received, waves, table, outer_cos,
    outer_sin, factor, grid_field, out, fourier, twisted, samples, tables, ready
):
    step = pl.program_id(0)

    def fetch(row):
        return pltpu.make_async_copy(table.at[row], tables.at[row], ready.at[row])

    @pl.when(step == 0)
    def _():
        for row in range(NB):
            fetch(row).start()
        for g in range(GROUPS):
            items = []
            for src in range(NB):
                block = received[src, g].astype(F32)
                items.append((block[:, :128], block[:, 128:]))
            for row, (lo, hi) in enumerate(exchange_chunks(items, 16)):
                fourier[row, :, 256 * g : 256 * g + 128] = lo
                fourier[row, :, 256 * g + 128 : 256 * g + 256] = hi

    lane = lax.broadcasted_iota(jnp.int32, (1, 256), 1)
    sign = jnp.where((lane & 1) == 1, F32(-1.0), F32(1.0))

    def limits(r):
        lat = row_latitude[band[0] * NB + step * rows_per_step + r] & (points.shape[0] - 1)
        return points[lat], cutoffs[lat].astype(F32)

    def twist(r):
        cutoff = limits(r)[1]
        for t in range(5):
            lanes = slice(256 * t, 256 * (t + 1))
            wave = waves[:, lanes]
            kept = (wave <= cutoff).astype(F32)
            weight = kept * jnp.where(wave == 0.0, F32(1.0), F32(2.0))
            x = fourier[step * rows_per_step + r, :, lanes]
            crossed = swap_parts(x) * -weight
            x = x * (weight * sign)
            for b in range(11):
                cosine, sine = outer_cos[r, b : b + 1, lanes], outer_sin[r, b : b + 1, lanes]
                value = x * cosine + crossed * sine
                twisted[r, 16 * b : 16 * (b + 1), lanes] = value.astype(BF16)

    def inverse(r):
        count = limits(r)[0]
        row = step * rows_per_step + r
        fetch(row).wait()
        field = dot(twisted[r], tables[row], NT)
        for b in range(11):
            size = 256 if b < 10 else 128
            cut = slice(256 * b, 256 * b + size)
            value = jnp.where(lane + 256 * b < count, field[16 * b : 16 * (b + 1), :], 0.0)
            value = value.astype(BF16)[:, :size]
            grid_field[r, :, cut] = value
            scaled = value.astype(F32) * factor[r, :, cut]
            samples[r, 16 * b : 16 * (b + 1), :size] = scaled.astype(BF16)
        samples[r, 160:176, 128:] = jnp.zeros((16, 128), BF16)

    def direct(r):
        count, cutoff = limits(r)
        row = step * rows_per_step + r
        for t in range(5):
            lanes = slice(256 * t, 256 * (t + 1))
            kept = (waves[:, lanes] <= cutoff).astype(F32)
            scale = kept / jnp.full((1, 256), count.astype(F32))
            part = dot(samples[r], tables[row, :, lanes])
            total_cos = jnp.zeros((16, 256), F32)
            total_sin = jnp.zeros((16, 256), F32)
            for b in range(11):
                block = part[16 * b : 16 * (b + 1), :]
                total_cos = total_cos + block * outer_cos[r, b : b + 1, lanes]
                total_sin = total_sin + block * outer_sin[r, b : b + 1, lanes]
            value = sign * total_cos - swap_parts(total_sin)
            out[r, :, lanes] = (value * scale).astype(BF16)

    twist(0)
    for r in range(rows_per_step):
        if r + 1 < rows_per_step:
            twist(r + 1)
        inverse(r)
        if r > 0:
            direct(r - 1)
    direct(rows_per_step - 1)


def mix_kernel(vertical, received, out, levels, rows):
    block = received[...].reshape(256, WAVES)
    for t in range(10):
        levels[256 * t : 256 * (t + 1), :] = dot(vertical[...], block[:, 128 * t : 128 * (t + 1)])
    for t in range(10):
        for high in range(2):
            first = 256 * t + 8 * high
            items = [levels[pl.ds(first + l, 16, stride=16), :] for l in range(8)]
            for b, item in enumerate(exchange_lanes(items, 16)):
                start = 160 * (8 * (t % 2) + b) + 2 * (t // 2) + high
                rows[pl.ds(start, 16, stride=10), :] = item
    out[...] = rows[...].astype(BF16)


def final_kernel(
    truncation, band, slot_pair, lane_latitude, weights, received, legendre, out, rows, full_out, sent
):
    width = legendre.shape[1]
    rows[...] = received[...].astype(F32)
    target = lax.broadcasted_iota(jnp.int32, (256, 256), 0)
    lane = lax.broadcasted_iota(jnp.int32, (256, 256), 1)
    source = lane_latitude[...]
    wave = ((target >> 5) << 1) | (target & 1)
    turn = ((lane >> 4 == ((target >> 1) & 15)) & ((lane & 15) == wave)).astype(F32).astype(BF16)
    value = jnp.where((target >= 128) & (source >= 128), F32(-1.0), F32(1.0))
    fold = jnp.where((target & 127) == (source & 127), value, 0.0).astype(BF16)
    parts = []
    for g in range(GROUPS):
        halves = [rows[pl.ds(2 * g + h, 256, stride=10), :].astype(BF16) for h in (0, 1)]
        turned = dot(turn, jnp.concatenate(halves, 1), NT).astype(BF16)
        parts.append((dot(turned, fold, NT) * weights[...]).astype(BF16))
    copies = []
    for g in range(GROUPS):
        for s in range(4):
            slot = 4 * g + s
            own = parts[g][64 * s : 64 * (s + 1)]
            left = jnp.concatenate([own[:, :128], own[:, 128:]], 0)
            full = dot(left, legendre[slot], NT)
            first, odd = slot_columns(slot_pair[band[0] * 20 + slot], width, truncation)
            even_part = jnp.where(first, full[0:32], full[32:64])
            odd_part = jnp.where(first, full[64:96], full[96:128])
            chosen = jnp.where(odd == 0, even_part, odd_part)
            full_out[:, slot] = chosen.reshape(16, 2, width)
        cut = pl.ds(4 * g, 4)
        copies.append(pltpu.make_async_copy(full_out.at[:, cut], out.at[:, cut], sent.at[g]))
        copies[g].start()
    for copy in copies:
        copy.wait()


def whole(shape):
    return pl.BlockSpec(shape, lambda i: (0,) * len(shape))


SMEM = pl.BlockSpec(memory_space=pltpu.SMEM)
VMEM = pl.BlockSpec(memory_space=pltpu.VMEM)
HBM = pl.BlockSpec(memory_space=pltpu.HBM)


def cost(flops, size):
    return pl.CostEstimate(flops=flops, bytes_accessed=size, transcendentals=0)


def in_hbm(array):
    return pltpu.with_memory_space_constraint(array, pltpu.HBM)


def everywhere(message):
    pieces = message.reshape(ROWS // 2, 2, 128)
    pieces = lax.all_to_all(pieces, ("band", "lev"), split_axis=0, concat_axis=0, tiled=True)
    return pieces.reshape(ROWS, 128)


def per_device(
    spectral, legendre, weights, vertical, grid_factor, points, cutoffs, row_latitude, slot_pair
):
    band = lax.axis_index("band").astype(jnp.int32).reshape(1)
    truncation = 2 * slot_pair.shape[0] - 1
    width = spectral.shape[3]
    row_width = grid_factor.shape[1]
    by_slot = spectral.transpose(0, 2, 1, 3)
    legendre = legendre.transpose(0, 2, 1)
    lane_latitude = row_latitude.reshape(NB, NB).T.reshape(1, 256)
    pairs = slot_pair.reshape(NB, GROUPS, 4).transpose(1, 0, 2)
    waves = jnp.stack([pairs, truncation - pairs], -1)
    waves = jnp.broadcast_to(waves[..., None], waves.shape + (2,)).reshape(1, WAVES).astype(F32)

    message = pl.pallas_call(
        lambda *refs: send_kernel(truncation, *refs),
        in_specs=[SMEM, SMEM, VMEM, HBM, HBM],
        out_specs=HBM,
        out_shape=pltpu.HBM((NB, GROUPS, 16, 256), BF16),
        scratch_shapes=[
            pltpu.VMEM((GROUPS, 256, 256), BF16),
            pltpu.VMEM((GROUPS, 2, 256, 128), F32),
            pltpu.VMEM(by_slot.shape, BF16),
            pltpu.VMEM(legendre.shape, BF16),
            pltpu.VMEM((NB, GROUPS, 16, 256), BF16),
            pltpu.SemaphoreType.DMA((GROUPS + 1,)),
            pltpu.SemaphoreType.DMA((GROUPS,)),
        ],
        compiler_params=params(),
        cost_estimate=cost(2 * 20 * 128 * 768 * 128, 5_000_000),
        name="legendre_send",
    )(band, slot_pair, lane_latitude, in_hbm(by_slot), in_hbm(legendre))
    received = lax.all_to_all(message, "band", split_axis=0, concat_axis=0, tiled=True)

    per_step = 2
    table, outer_cos, outer_sin = pl.pallas_call(
        lambda *refs: table_kernel(per_step, *refs),
        grid=(NB // per_step,),
        in_specs=[SMEM, SMEM, SMEM, whole((1, WAVES))],
        out_specs=[
            pl.BlockSpec((per_step, 256, WAVES), lambda i: (i, 0, 0)),
            pl.BlockSpec((per_step, 16, WAVES), lambda i: (i, 0, 0)),
            pl.BlockSpec((per_step, 16, WAVES), lambda i: (i, 0, 0)),
        ],
        out_shape=[
            pltpu.HBM((NB, 256, WAVES), BF16),
            jax.ShapeDtypeStruct((NB, 16, WAVES), F32),
            jax.ShapeDtypeStruct((NB, 16, WAVES), F32),
        ],
        scratch_shapes=[pltpu.VMEM((4, 16, WAVES), F32)],
        compiler_params=params(),
        cost_estimate=cost(16 * 256 * 1280 * 20, 14_000_000),
        name="phase_tables",
    )(band, row_latitude, points, waves)

    per_step = 4
    factor = grid_factor.astype(F32).reshape(NB, 1, row_width)
    grid_field, harmonic = pl.pallas_call(
        lambda *refs: rows_kernel(per_step, *refs),
        grid=(NB // per_step,),
        in_specs=[
            SMEM, SMEM, SMEM, SMEM,
            whole((NB, GROUPS, 16, 256)),
            whole((1, WAVES)),
            HBM,
            pl.BlockSpec((per_step, 16, WAVES), lambda i: (i, 0, 0)),
            pl.BlockSpec((per_step, 16, WAVES), lambda i: (i, 0, 0)),
            pl.BlockSpec((per_step, 1, row_width), lambda i: (i, 0, 0)),
        ],
        out_specs=[
            pl.BlockSpec((per_step, 16, row_width), lambda i: (i, 0, 0)),
            pl.BlockSpec((per_step, 16, WAVES), lambda i: (i, 0, 0)),
        ],
        out_shape=[
            jax.ShapeDtypeStruct((NB, 16, row_width), BF16),
            jax.ShapeDtypeStruct((NB, 16, WAVES), BF16),
        ],
        scratch_shapes=[
            pltpu.VMEM((NB, 16, WAVES), F32),
            pltpu.VMEM((per_step, 176, WAVES), BF16),
            pltpu.VMEM((per_step, 176, 256), BF16),
            pltpu.VMEM((NB, 256, WAVES), BF16),
            pltpu.SemaphoreType.DMA((NB,)),
        ],
        compiler_params=params(32),
        cost_estimate=cost(4 * 16 * 176 * 1280 * 256, 17_000_000),
        name="grid_rows",
    )(band, row_latitude, points, cutoffs, received, waves, in_hbm(table), outer_cos, outer_sin,
      factor)

    levels_in = lax.all_to_all(harmonic, "lev", split_axis=0, concat_axis=0, tiled=True)
    outgoing = pl.pallas_call(
        mix_kernel,
        in_specs=[VMEM, VMEM],
        out_specs=VMEM,
        out_shape=jax.ShapeDtypeStruct((ROWS, 128), BF16),
        scratch_shapes=[pltpu.VMEM((ROWS, 128), F32), pltpu.VMEM((ROWS, 128), F32)],
        compiler_params=params(),
        cost_estimate=cost(2 * 256 * 256 * 1280, 1_400_000),
        name="vertical_mix",
    )(vertical, levels_in)
    returned = everywhere(outgoing)

    round_trip = pl.pallas_call(
        lambda *refs: final_kernel(truncation, *refs),
        in_specs=[SMEM, SMEM, VMEM, VMEM, VMEM, VMEM],
        out_specs=HBM,
        out_shape=jax.ShapeDtypeStruct((16, 20, 2, width), F32),
        scratch_shapes=[
            pltpu.VMEM((ROWS, 128), F32),
            pltpu.VMEM((16, 20, 2, width), F32),
            pltpu.SemaphoreType.DMA((GROUPS,)),
        ],
        compiler_params=params(),
        cost_estimate=cost(2 * 20 * 128 * 768 * 128, 6_000_000),
        name="legendre_return",
    )(
        band, slot_pair, row_latitude.reshape(1, 256),
        jnp.concatenate([weights, weights]).reshape(1, 256), returned, legendre,
    )
    return (grid_field, round_trip.transpose(0, 2, 1, 3))


def solution(mesh):
    in_specs = (
        P("lev", None, "band", None),
        P("band", None, None),
        P(),
        P(),
        P("band", None),
        P(),
        P(),
        P(),
        P(),
    )
    out_specs = (P("band", "lev", None), P("lev", None, "band", None))
    return jax.shard_map(
        per_device, mesh=mesh, in_specs=in_specs, out_specs=out_specs, check_vma=False
    )
```

```python
import math

import jax
import jax.numpy as jnp
from jax import lax
from jax.experimental import pallas as pl
from jax.experimental.pallas import tpu as pltpu
from jax.sharding import PartitionSpec as P

F32, BF16 = jnp.float32, jnp.bfloat16
NB = 16
GROUPS = 5
ROWS = 2560
WAVES = 1280
COS = (1.0, -19.739208221435547, 64.93938446044922, -85.45658111572266,
       60.241241455078125, -26.39919662475586, 7.783571243286133, -1.4335278272628784)
SIN = (6.2831854820251465, -41.34170150756836, 81.6052474975586, -76.70577239990234,
       42.05741882324219, -15.084507942199707, 3.775092124938965, -0.6134149432182312)
NT = (((1,), (1,)), ((), ()))


def params(limit=24):
    return pltpu.CompilerParams(vmem_limit_bytes=limit * 1024 * 1024)


def dot(a, b, dims=(((1,), (0,)), ((), ()))):
    return lax.dot_general(a, b, dims, preferred_element_type=F32)


def exchange_chunks(items, width):
    items = list(items)
    lane = lax.broadcasted_iota(jnp.int32, items[0][0].shape, 1)
    for level in range(4):
        step = 1 << level
        shift = width * step
        for low in range(16):
            if low & step:
                continue
            a, b = items[low], items[low + step]
            if shift == 128:
                items[low], items[low + step] = (a[0], b[0]), (a[1], b[1])
                continue
            keep = (lane & shift) == 0
            items[low] = tuple(jnp.where(keep, a[h], pltpu.roll(b[h], shift, 1)) for h in (0, 1))
            items[low + step] = tuple(
                jnp.where(keep, pltpu.roll(a[h], 128 - shift, 1), b[h]) for h in (0, 1)
            )
    return items


def exchange_lanes(items, width):
    items = list(items)
    lane = lax.broadcasted_iota(jnp.int32, items[0].shape, 1)
    count = len(items)
    for level in range(count.bit_length() - 1):
        step = 1 << level
        shift = width * step
        keep = (lane & shift) == 0
        for low in range(count):
            if low & step:
                continue
            a, b = items[low], items[low + step]
            items[low] = jnp.where(keep, a, pltpu.roll(b, shift, 1))
            items[low + step] = jnp.where(keep, pltpu.roll(a, 128 - shift, 1), b)
    return items


def swap_parts(x):
    lane = lax.broadcasted_iota(jnp.int32, (x.shape[0], 128), 1)
    even = (lane & 1) == 0
    pieces = []
    for t in range(x.shape[1] // 128):
        piece = x[:, 128 * t : 128 * (t + 1)]
        pieces.append(jnp.where(even, pltpu.roll(piece, 127, 1), pltpu.roll(piece, 1, 1)))
    return jnp.concatenate(pieces, 1)


def slot_columns(pair, width, truncation):
    column = lax.broadcasted_iota(jnp.int32, (1, width), 1)
    split = truncation + 1 - pair
    first = column < split
    odd = jnp.where(first, column, column - split) & 1
    return first, odd


def table_kernel(rows_per_step, band, row_latitude, points, waves, table, outer_cos, outer_sin, seeds):
    step = pl.program_id(0)
    wave = waves[...]
    imag = (lax.broadcasted_iota(jnp.int32, (1, WAVES), 1) & 1) == 1
    index = lax.broadcasted_iota(jnp.int32, (16, WAVES), 0).astype(F32)
    for r in range(rows_per_step):
        lat = row_latitude[band[0] * NB + step * rows_per_step + r] & (points.shape[0] - 1)
        count = jnp.full((1, WAVES), points[lat].astype(F32))
        inverse = 1.0 / count

        def circle(stride):
            product = (wave * stride) * index
            turns = jnp.floor(product * inverse + 0.5)
            y = (product - turns * count) * inverse
            z = y * y
            c = jnp.full_like(z, COS[-1])
            s = jnp.full_like(z, SIN[-1])
            for k in range(6, -1, -1):
                c = c * z + COS[k]
                s = s * z + SIN[k]
            return c, s * y

        c1, s1 = circle(1.0)
        c2, s2 = circle(16.0)
        seeds[0] = jnp.where(imag, s2, c2)
        seeds[1] = jnp.where(imag, -c2, s2)
        seeds[2] = c1
        seeds[3] = s1
        c3, s3 = circle(256.0)
        outer_cos[r] = c3
        outer_sin[r] = s3
        for t in range(5):
            lanes = slice(256 * t, 256 * (t + 1))
            c1, s1 = seeds[2, :, lanes], seeds[3, :, lanes]
            for a in range(16):
                value = seeds[0, a : a + 1, lanes] * c1 - seeds[1, a : a + 1, lanes] * s1
                table[r, 16 * a : 16 * (a + 1), lanes] = value.astype(BF16)


def send_kernel(
    truncation, band, all_pairs, lane_latitude, spectral, legendre, out, sums, spread, spectral_in,
    legendre_in, messages, slot_pair, ready, sent
):
    width = spectral.shape[-1]
    slots = pltpu.make_async_copy(all_pairs, slot_pair, ready.at[GROUPS + 1])
    slots.start()
    whole_spectral = pltpu.make_async_copy(spectral, spectral_in, ready.at[GROUPS])
    whole_spectral.start()
    copies = []
    for g in range(GROUPS):
        cut = pl.ds(4 * g, 4)
        copies.append(pltpu.make_async_copy(legendre.at[cut], legendre_in.at[cut], ready.at[g]))
        copies[g].start()
    index = lax.broadcasted_iota(jnp.int32, (256, 256), 0)
    lane = lax.broadcasted_iota(jnp.int32, (256, 256), 1)
    place = (index == lane_latitude[...]).astype(F32).astype(BF16)
    by_row = (index == ((lane & 15) << 4 | lane >> 4)).astype(F32).astype(BF16)
    place = dot(place, by_row).astype(BF16)
    slots.wait()
    whole_spectral.wait()
    for g in range(GROUPS):
        copies[g].wait()
        values = []
        for s in range(4 * g, 4 * g + 4):
            first, odd = slot_columns(slot_pair[band[0] * 20 + s], width, truncation)
            one = first.astype(F32)
            sign = 1.0 - 2.0 * odd.astype(F32)
            x = spectral_in[:, s].reshape(32, width)
            picks = [one, 1.0 - one, one * sign, (1.0 - one) * sign]
            left = jnp.concatenate([x * p.astype(BF16) for p in picks], 0)
            values.append(dot(left, legendre_in[s]).astype(BF16))
        for s in range(4):
            sums[g, 64 * s : 64 * (s + 1), :128] = values[s][:64]
            sums[g, 64 * s : 64 * (s + 1), 128:] = values[s][64:]
    for g in range(GROUPS):
        placed = dot(sums[g], place)
        spread[g, 0] = placed[:, :128]
        spread[g, 1] = placed[:, 128:]
        items = []
        for u in range(16):
            at = pl.ds(32 * (u >> 1) + (u & 1), 16, stride=2)
            items.append((spread[g, 0, at, :], spread[g, 1, at, :]))
        for b, (lo, hi) in enumerate(exchange_chunks(items, 1)):
            messages[b, g, :, :128] = lo.astype(BF16)
            messages[b, g, :, 128:] = hi.astype(BF16)
        cut = pl.ds(g, 1)
        copies[g] = pltpu.make_async_copy(messages.at[:, cut], out.at[:, cut], sent.at[g])
        copies[g].start()
    for copy in copies:
        copy.wait()


def rows_kernel(
    rows_per_step, band, row_latitude, points, cutoffs, received, waves, table, outer_cos,
    outer_sin, factor, grid_field, out, fourier, twisted, samples, tables, ready
):
    step = pl.program_id(0)

    def fetch(row):
        return pltpu.make_async_copy(table.at[row], tables.at[row], ready.at[row])

    @pl.when(step == 0)
    def _():
        for row in range(rows_per_step):
            fetch(row).start()
        for g in range(GROUPS):
            items = []
            for src in range(NB):
                block = received[src, g].astype(F32)
                items.append((block[:, :128], block[:, 128:]))
            for row, (lo, hi) in enumerate(exchange_chunks(items, 16)):
                fourier[row, :, 256 * g : 256 * g + 128] = lo
                fourier[row, :, 256 * g + 128 : 256 * g + 256] = hi

    @pl.when(step + 1 < pl.num_programs(0))
    def _():
        for r in range(rows_per_step):
            fetch((step + 1) * rows_per_step + r).start()

    lane = lax.broadcasted_iota(jnp.int32, (1, 256), 1)
    sign = jnp.where((lane & 1) == 1, F32(-1.0), F32(1.0))

    def limits(r):
        lat = row_latitude[band[0] * NB + step * rows_per_step + r] & (points.shape[0] - 1)
        return points[lat], cutoffs[lat].astype(F32)

    def twist(r):
        cutoff = limits(r)[1]
        for t in range(5):
            lanes = slice(256 * t, 256 * (t + 1))
            wave = waves[:, lanes]
            kept = (wave <= cutoff).astype(F32)
            weight = kept * jnp.where(wave == 0.0, F32(1.0), F32(2.0))
            x = fourier[step * rows_per_step + r, :, lanes]
            crossed = swap_parts(x) * -weight
            x = x * (weight * sign)
            for b in range(11):
                cosine, sine = outer_cos[r, b : b + 1, lanes], outer_sin[r, b : b + 1, lanes]
                value = x * cosine + crossed * sine
                twisted[r, 16 * b : 16 * (b + 1), lanes] = value.astype(BF16)

    def inverse(r):
        count = limits(r)[0]
        row = step * rows_per_step + r
        fetch(row).wait()
        field = dot(twisted[r], tables[row], NT)
        for b in range(11):
            size = 256 if b < 10 else 128
            cut = slice(256 * b, 256 * b + size)
            value = jnp.where(lane + 256 * b < count, field[16 * b : 16 * (b + 1), :], 0.0)
            value = value.astype(BF16)[:, :size]
            grid_field[r, :, cut] = value
            scaled = value.astype(F32) * factor[r, :, cut]
            samples[r, 16 * b : 16 * (b + 1), :size] = scaled.astype(BF16)
        samples[r, 160:176, 128:] = jnp.zeros((16, 128), BF16)

    def direct(r):
        count, cutoff = limits(r)
        row = step * rows_per_step + r
        for t in range(5):
            lanes = slice(256 * t, 256 * (t + 1))
            kept = (waves[:, lanes] <= cutoff).astype(F32)
            scale = kept / jnp.full((1, 256), count.astype(F32))
            part = dot(samples[r], tables[row, :, lanes])
            total_cos = jnp.zeros((16, 256), F32)
            total_sin = jnp.zeros((16, 256), F32)
            for b in range(11):
                block = part[16 * b : 16 * (b + 1), :]
                total_cos = total_cos + block * outer_cos[r, b : b + 1, lanes]
                total_sin = total_sin + block * outer_sin[r, b : b + 1, lanes]
            value = sign * total_cos - swap_parts(total_sin)
            out[r, :, lanes] = (value * scale).astype(BF16)

    twist(0)
    for r in range(rows_per_step):
        if r + 1 < rows_per_step:
            twist(r + 1)
        inverse(r)
        if r > 0:
            direct(r - 1)
    direct(rows_per_step - 1)


def mix_kernel(vertical, received, out, levels, rows):
    block = received[...].reshape(256, WAVES)
    for t in range(10):
        levels[256 * t : 256 * (t + 1), :] = dot(vertical[...], block[:, 128 * t : 128 * (t + 1)])
    for t in range(10):
        for high in range(2):
            first = 256 * t + 8 * high
            items = [levels[pl.ds(first + l, 16, stride=16), :] for l in range(8)]
            for b, item in enumerate(exchange_lanes(items, 16)):
                start = 160 * (8 * (t % 2) + b) + 2 * (t // 2) + high
                rows[pl.ds(start, 16, stride=10), :] = item
    out[...] = rows[...].astype(BF16)


def final_kernel(
    truncation, band, slot_pair, lane_latitude, weights, received, legendre, out, rows, full_out, sent
):
    width = legendre.shape[1]
    rows[...] = received[...].astype(F32)
    target = lax.broadcasted_iota(jnp.int32, (256, 256), 0)
    lane = lax.broadcasted_iota(jnp.int32, (256, 256), 1)
    source = lane_latitude[...]
    wave = ((target >> 5) << 1) | (target & 1)
    turn = ((lane >> 4 == ((target >> 1) & 15)) & ((lane & 15) == wave)).astype(F32).astype(BF16)
    value = jnp.where((target >= 128) & (source >= 128), F32(-1.0), F32(1.0))
    fold = jnp.where((target & 127) == (source & 127), value, 0.0).astype(BF16)
    doubled = jnp.concatenate([weights[...], weights[...]], 1)
    parts = []
    for g in range(GROUPS):
        halves = [rows[pl.ds(2 * g + h, 256, stride=10), :].astype(BF16) for h in (0, 1)]
        turned = dot(turn, jnp.concatenate(halves, 1), NT).astype(BF16)
        parts.append((dot(turned, fold, NT) * doubled).astype(BF16))
    copies = []
    for g in range(GROUPS):
        for s in range(4):
            slot = 4 * g + s
            own = parts[g][64 * s : 64 * (s + 1)]
            left = jnp.concatenate([own[:, :128], own[:, 128:]], 0)
            full = dot(left, legendre[slot], NT)
            first, odd = slot_columns(slot_pair[band[0] * 20 + slot], width, truncation)
            even_part = jnp.where(first, full[0:32], full[32:64])
            odd_part = jnp.where(first, full[64:96], full[96:128])
            chosen = jnp.where(odd == 0, even_part, odd_part)
            full_out[:, slot] = chosen.reshape(16, 2, width)
        cut = pl.ds(4 * g, 4)
        copies.append(pltpu.make_async_copy(full_out.at[:, cut], out.at[:, cut], sent.at[g]))
        copies[g].start()
    for copy in copies:
        copy.wait()


def whole(shape):
    return pl.BlockSpec(shape, lambda i: (0,) * len(shape))


SMEM = pl.BlockSpec(memory_space=pltpu.SMEM)
VMEM = pl.BlockSpec(memory_space=pltpu.VMEM)
HBM = pl.BlockSpec(memory_space=pltpu.HBM)


def cost(flops, size):
    return pl.CostEstimate(flops=flops, bytes_accessed=size, transcendentals=0)


def in_hbm(array):
    return pltpu.with_memory_space_constraint(array, pltpu.HBM)


def everywhere(message):
    pieces = message.reshape(ROWS // 2, 2, 128)
    pieces = lax.all_to_all(pieces, ("band", "lev"), split_axis=0, concat_axis=0, tiled=True)
    return pieces.reshape(ROWS, 128)


def per_device(
    spectral, legendre, weights, vertical, grid_factor, points, cutoffs, row_latitude, slot_pair
):
    band = lax.axis_index("band").astype(jnp.int32).reshape(1)
    truncation = 2 * slot_pair.shape[0] - 1
    width = spectral.shape[3]
    row_width = grid_factor.shape[1]
    by_slot = spectral.transpose(0, 2, 1, 3)
    legendre = legendre.transpose(0, 2, 1)
    lane_latitude = row_latitude.reshape(1, 256)
    pairs = slot_pair.reshape(NB, GROUPS, 4).transpose(1, 0, 2)
    waves = jnp.stack([pairs, truncation - pairs], -1)
    waves = jnp.broadcast_to(waves[..., None], waves.shape + (2,)).reshape(1, WAVES).astype(F32)

    message = pl.pallas_call(
        lambda *refs: send_kernel(truncation, *refs),
        in_specs=[SMEM, HBM, VMEM, HBM, HBM],
        out_specs=HBM,
        out_shape=pltpu.HBM((NB, GROUPS, 16, 256), BF16),
        scratch_shapes=[
            pltpu.VMEM((GROUPS, 256, 256), BF16),
            pltpu.VMEM((GROUPS, 2, 256, 128), F32),
            pltpu.VMEM(by_slot.shape, BF16),
            pltpu.VMEM(legendre.shape, BF16),
            pltpu.VMEM((NB, GROUPS, 16, 256), BF16),
            pltpu.SMEM(slot_pair.shape, jnp.int32),
            pltpu.SemaphoreType.DMA((GROUPS + 2,)),
            pltpu.SemaphoreType.DMA((GROUPS,)),
        ],
        compiler_params=params(),
        cost_estimate=cost(2 * 20 * 128 * 768 * 128, 5_000_000),
        name="legendre_send",
    )(band, in_hbm(slot_pair), lane_latitude, in_hbm(by_slot), in_hbm(legendre))
    received = lax.all_to_all(message, "band", split_axis=0, concat_axis=0, tiled=True)

    per_step = 2
    table, outer_cos, outer_sin = pl.pallas_call(
        lambda *refs: table_kernel(per_step, *refs),
        grid=(NB // per_step,),
        in_specs=[SMEM, SMEM, SMEM, whole((1, WAVES))],
        out_specs=[
            pl.BlockSpec((per_step, 256, WAVES), lambda i: (i, 0, 0)),
            pl.BlockSpec((per_step, 16, WAVES), lambda i: (i, 0, 0)),
            pl.BlockSpec((per_step, 16, WAVES), lambda i: (i, 0, 0)),
        ],
        out_shape=[
            pltpu.HBM((NB, 256, WAVES), BF16),
            jax.ShapeDtypeStruct((NB, 16, WAVES), F32),
            jax.ShapeDtypeStruct((NB, 16, WAVES), F32),
        ],
        scratch_shapes=[pltpu.VMEM((4, 16, WAVES), F32)],
        compiler_params=params(),
        cost_estimate=cost(16 * 256 * 1280 * 20, 14_000_000),
        name="phase_tables",
    )(band, row_latitude, points, waves)

    per_step = 4
    factor = grid_factor.astype(F32).reshape(NB, 1, row_width)
    grid_field, harmonic = pl.pallas_call(
        lambda *refs: rows_kernel(per_step, *refs),
        grid=(NB // per_step,),
        in_specs=[
            SMEM, SMEM, SMEM, SMEM,
            whole((NB, GROUPS, 16, 256)),
            whole((1, WAVES)),
            HBM,
            pl.BlockSpec((per_step, 16, WAVES), lambda i: (i, 0, 0)),
            pl.BlockSpec((per_step, 16, WAVES), lambda i: (i, 0, 0)),
            pl.BlockSpec((per_step, 1, row_width), lambda i: (i, 0, 0)),
        ],
        out_specs=[
            pl.BlockSpec((per_step, 16, row_width), lambda i: (i, 0, 0)),
            pl.BlockSpec((per_step, 16, WAVES), lambda i: (i, 0, 0)),
        ],
        out_shape=[
            jax.ShapeDtypeStruct((NB, 16, row_width), BF16),
            jax.ShapeDtypeStruct((NB, 16, WAVES), BF16),
        ],
        scratch_shapes=[
            pltpu.VMEM((NB, 16, WAVES), F32),
            pltpu.VMEM((per_step, 176, WAVES), BF16),
            pltpu.VMEM((per_step, 176, 256), BF16),
            pltpu.VMEM((NB, 256, WAVES), BF16),
            pltpu.SemaphoreType.DMA((NB,)),
        ],
        compiler_params=params(32),
        cost_estimate=cost(4 * 16 * 176 * 1280 * 256, 17_000_000),
        name="grid_rows",
    )(band, row_latitude, points, cutoffs, received, waves, in_hbm(table), outer_cos, outer_sin,
      factor)

    levels_in = lax.all_to_all(harmonic, "lev", split_axis=0, concat_axis=0, tiled=True)
    outgoing = pl.pallas_call(
        mix_kernel,
        in_specs=[VMEM, VMEM],
        out_specs=VMEM,
        out_shape=jax.ShapeDtypeStruct((ROWS, 128), BF16),
        scratch_shapes=[pltpu.VMEM((ROWS, 128), F32), pltpu.VMEM((ROWS, 128), F32)],
        compiler_params=params(),
        cost_estimate=cost(2 * 256 * 256 * 1280, 1_400_000),
        name="vertical_mix",
    )(vertical, levels_in)
    returned = everywhere(outgoing)

    round_trip = pl.pallas_call(
        lambda *refs: final_kernel(truncation, *refs),
        in_specs=[SMEM, SMEM, VMEM, VMEM, VMEM, VMEM],
        out_specs=HBM,
        out_shape=jax.ShapeDtypeStruct((16, 20, 2, width), F32),
        scratch_shapes=[
            pltpu.VMEM((ROWS, 128), F32),
            pltpu.VMEM((16, 20, 2, width), F32),
            pltpu.SemaphoreType.DMA((GROUPS,)),
        ],
        compiler_params=params(),
        cost_estimate=cost(2 * 20 * 128 * 768 * 128, 6_000_000),
        name="legendre_return",
    )(
        band, slot_pair, lane_latitude, weights.reshape(1, 128), returned, legendre,
    )
    return (grid_field, round_trip.transpose(0, 2, 1, 3))


def solution(mesh):
    in_specs = (
        P("lev", None, "band", None),
        P("band", None, None),
        P(),
        P(),
        P("band", None),
        P(),
        P(),
        P(),
        P(),
    )
    out_specs = (P("band", "lev", None), P("lev", None, "band", None))
    return jax.shard_map(
        per_device, mesh=mesh, in_specs=in_specs, out_specs=out_specs, check_vma=False
    )
```

```python
import math

import jax
import jax.numpy as jnp
from jax import lax
from jax.experimental import pallas as pl
from jax.experimental.pallas import tpu as pltpu
from jax.sharding import PartitionSpec as P

F32, BF16 = jnp.float32, jnp.bfloat16
NB = 16
GROUPS = 5
ROWS = 2560
WAVES = 1280
COS = (1.0, -19.739208221435547, 64.93938446044922, -85.45658111572266,
       60.241241455078125, -26.39919662475586, 7.783571243286133, -1.4335278272628784)
SIN = (6.2831854820251465, -41.34170150756836, 81.6052474975586, -76.70577239990234,
       42.05741882324219, -15.084507942199707, 3.775092124938965, -0.6134149432182312)
NT = (((1,), (1,)), ((), ()))


def params(limit=24):
    return pltpu.CompilerParams(vmem_limit_bytes=limit * 1024 * 1024)


def dot(a, b, dims=(((1,), (0,)), ((), ()))):
    return lax.dot_general(a, b, dims, preferred_element_type=F32)


def exchange_chunks(items, width):
    items = list(items)
    lane = lax.broadcasted_iota(jnp.int32, items[0][0].shape, 1)
    for level in range(4):
        step = 1 << level
        shift = width * step
        for low in range(16):
            if low & step:
                continue
            a, b = items[low], items[low + step]
            if shift == 128:
                items[low], items[low + step] = (a[0], b[0]), (a[1], b[1])
                continue
            keep = (lane & shift) == 0
            items[low] = tuple(jnp.where(keep, a[h], pltpu.roll(b[h], shift, 1)) for h in (0, 1))
            items[low + step] = tuple(
                jnp.where(keep, pltpu.roll(a[h], 128 - shift, 1), b[h]) for h in (0, 1)
            )
    return items


def exchange_lanes(items, width):
    items = list(items)
    lane = lax.broadcasted_iota(jnp.int32, items[0].shape, 1)
    count = len(items)
    for level in range(count.bit_length() - 1):
        step = 1 << level
        shift = width * step
        keep = (lane & shift) == 0
        for low in range(count):
            if low & step:
                continue
            a, b = items[low], items[low + step]
            items[low] = jnp.where(keep, a, pltpu.roll(b, shift, 1))
            items[low + step] = jnp.where(keep, pltpu.roll(a, 128 - shift, 1), b)
    return items


def swap_parts(x):
    lane = lax.broadcasted_iota(jnp.int32, (x.shape[0], 128), 1)
    even = (lane & 1) == 0
    pieces = []
    for t in range(x.shape[1] // 128):
        piece = x[:, 128 * t : 128 * (t + 1)]
        pieces.append(jnp.where(even, pltpu.roll(piece, 127, 1), pltpu.roll(piece, 1, 1)))
    return jnp.concatenate(pieces, 1)


def slot_columns(pair, width, truncation):
    column = lax.broadcasted_iota(jnp.int32, (1, width), 1)
    split = truncation + 1 - pair
    first = column < split
    odd = jnp.where(first, column, column - split) & 1
    return first, odd


def table_kernel(rows_per_step, band, row_latitude, points, waves, table, outer_cos, outer_sin, seeds):
    step = pl.program_id(0)
    wave = waves[...]
    imag = (lax.broadcasted_iota(jnp.int32, (1, WAVES), 1) & 1) == 1
    index = lax.broadcasted_iota(jnp.int32, (16, WAVES), 0).astype(F32)
    for r in range(rows_per_step):
        lat = row_latitude[band[0] * NB + step * rows_per_step + r] & (points.shape[0] - 1)
        count = jnp.full((1, WAVES), points[lat].astype(F32))
        inverse = 1.0 / count

        def circle(stride):
            product = (wave * stride) * index
            turns = jnp.floor(product * inverse + 0.5)
            y = (product - turns * count) * inverse
            z = y * y
            c = jnp.full_like(z, COS[-1])
            s = jnp.full_like(z, SIN[-1])
            for k in range(6, -1, -1):
                c = c * z + COS[k]
                s = s * z + SIN[k]
            return c, s * y

        c1, s1 = circle(1.0)
        c2, s2 = circle(16.0)
        seeds[0] = jnp.where(imag, s2, c2)
        seeds[1] = jnp.where(imag, -c2, s2)
        seeds[2] = c1
        seeds[3] = s1
        c3, s3 = circle(256.0)
        outer_cos[r] = c3
        outer_sin[r] = s3
        for t in range(5):
            lanes = slice(256 * t, 256 * (t + 1))
            c1, s1 = seeds[2, :, lanes], seeds[3, :, lanes]
            for a in range(16):
                value = seeds[0, a : a + 1, lanes] * c1 - seeds[1, a : a + 1, lanes] * s1
                table[r, 16 * a : 16 * (a + 1), lanes] = value.astype(BF16)


def send_kernel(
    truncation, band, all_pairs, latitudes, spectral, legendre, out, sums, spread, spectral_in,
    legendre_in, messages, slot_pair, lane_latitude, ready, sent
):
    width = spectral.shape[-1]
    slots = pltpu.make_async_copy(all_pairs, slot_pair, ready.at[GROUPS + 1])
    slots.start()
    rows = pltpu.make_async_copy(latitudes, lane_latitude, ready.at[GROUPS + 2])
    rows.start()
    whole_spectral = pltpu.make_async_copy(spectral, spectral_in, ready.at[GROUPS])
    whole_spectral.start()
    copies = []
    for g in range(GROUPS):
        cut = pl.ds(4 * g, 4)
        copies.append(pltpu.make_async_copy(legendre.at[cut], legendre_in.at[cut], ready.at[g]))
        copies[g].start()
    index = lax.broadcasted_iota(jnp.int32, (256, 256), 0)
    lane = lax.broadcasted_iota(jnp.int32, (256, 256), 1)
    rows.wait()
    place = (index == lane_latitude[...]).astype(F32).astype(BF16)
    by_row = (index == ((lane & 15) << 4 | lane >> 4)).astype(F32).astype(BF16)
    place = dot(place, by_row).astype(BF16)
    slots.wait()
    whole_spectral.wait()
    for g in range(GROUPS):
        copies[g].wait()
        values = []
        for s in range(4 * g, 4 * g + 4):
            first, odd = slot_columns(slot_pair[band[0] * 20 + s], width, truncation)
            one = first.astype(F32)
            sign = 1.0 - 2.0 * odd.astype(F32)
            x = spectral_in[:, s].reshape(32, width)
            picks = [one, 1.0 - one, one * sign, (1.0 - one) * sign]
            left = jnp.concatenate([x * p.astype(BF16) for p in picks], 0)
            values.append(dot(left, legendre_in[s]).astype(BF16))
        for s in range(4):
            sums[g, 64 * s : 64 * (s + 1), :128] = values[s][:64]
            sums[g, 64 * s : 64 * (s + 1), 128:] = values[s][64:]
    for g in range(GROUPS):
        placed = dot(sums[g], place)
        spread[g, 0] = placed[:, :128]
        spread[g, 1] = placed[:, 128:]
        items = []
        for u in range(16):
            at = pl.ds(32 * (u >> 1) + (u & 1), 16, stride=2)
            items.append((spread[g, 0, at, :], spread[g, 1, at, :]))
        for b, (lo, hi) in enumerate(exchange_chunks(items, 1)):
            messages[b, g, :, :128] = lo.astype(BF16)
            messages[b, g, :, 128:] = hi.astype(BF16)
        cut = pl.ds(g, 1)
        copies[g] = pltpu.make_async_copy(messages.at[:, cut], out.at[:, cut], sent.at[g])
        copies[g].start()
    for copy in copies:
        copy.wait()


def rows_kernel(
    rows_per_step, band, row_latitude, points, cutoffs, received, waves, table, outer_cos,
    outer_sin, factor, grid_field, out, fourier, twisted, samples
):
    step = pl.program_id(0)

    @pl.when(step == 0)
    def _():
        for g in range(GROUPS):
            items = []
            for src in range(NB):
                block = received[src, g].astype(F32)
                items.append((block[:, :128], block[:, 128:]))
            for row, (lo, hi) in enumerate(exchange_chunks(items, 16)):
                fourier[row, :, 256 * g : 256 * g + 128] = lo
                fourier[row, :, 256 * g + 128 : 256 * g + 256] = hi

    lane = lax.broadcasted_iota(jnp.int32, (1, 256), 1)
    sign = jnp.where((lane & 1) == 1, F32(-1.0), F32(1.0))

    def limits(r):
        lat = row_latitude[band[0] * NB + step * rows_per_step + r] & (points.shape[0] - 1)
        return points[lat], cutoffs[lat].astype(F32)

    def twist(r):
        cutoff = limits(r)[1]
        for t in range(5):
            lanes = slice(256 * t, 256 * (t + 1))
            wave = waves[:, lanes]
            kept = (wave <= cutoff).astype(F32)
            weight = kept * jnp.where(wave == 0.0, F32(1.0), F32(2.0))
            x = fourier[step * rows_per_step + r, :, lanes]
            crossed = swap_parts(x) * -weight
            x = x * (weight * sign)
            for b in range(11):
                cosine, sine = outer_cos[r, b : b + 1, lanes], outer_sin[r, b : b + 1, lanes]
                value = x * cosine + crossed * sine
                twisted[r, 16 * b : 16 * (b + 1), lanes] = value.astype(BF16)

    def inverse(r):
        count = limits(r)[0]
        field = dot(twisted[r], table[r], NT)
        for b in range(11):
            size = 256 if b < 10 else 128
            cut = slice(256 * b, 256 * b + size)
            value = jnp.where(lane + 256 * b < count, field[16 * b : 16 * (b + 1), :], 0.0)
            value = value.astype(BF16)[:, :size]
            grid_field[r, :, cut] = value
            scaled = value.astype(F32) * factor[r, :, cut]
            samples[r, 16 * b : 16 * (b + 1), :size] = scaled.astype(BF16)
        samples[r, 160:176, 128:] = jnp.zeros((16, 128), BF16)

    def direct(r):
        count, cutoff = limits(r)
        for t in range(5):
            lanes = slice(256 * t, 256 * (t + 1))
            kept = (waves[:, lanes] <= cutoff).astype(F32)
            scale = kept / jnp.full((1, 256), count.astype(F32))
            part = dot(samples[r], table[r, :, lanes])
            total_cos = jnp.zeros((16, 256), F32)
            total_sin = jnp.zeros((16, 256), F32)
            for b in range(11):
                block = part[16 * b : 16 * (b + 1), :]
                total_cos = total_cos + block * outer_cos[r, b : b + 1, lanes]
                total_sin = total_sin + block * outer_sin[r, b : b + 1, lanes]
            value = sign * total_cos - swap_parts(total_sin)
            out[r, :, lanes] = (value * scale).astype(BF16)

    twist(0)
    for r in range(rows_per_step):
        if r + 1 < rows_per_step:
            twist(r + 1)
        inverse(r)
        if r > 0:
            direct(r - 1)
    direct(rows_per_step - 1)


def mix_kernel(vertical, received, out, rows):
    index = lax.broadcasted_iota(jnp.int32, (256, 256), 0)
    lane = lax.broadcasted_iota(jnp.int32, (256, 256), 1)
    by_level = (((lane & 15) == index >> 4) & (lane >> 4 == (index & 15))).astype(F32).astype(BF16)
    matrix = dot(by_level, vertical[...]).astype(BF16)
    block = received[...].reshape(256, WAVES)
    values = []
    for t in range(5):
        value = dot(matrix, block[:, 256 * t : 256 * (t + 1)])
        values += [value[:, :128], value[:, 128:]]
    for t in range(10):
        for high in range(2):
            levels = range(128 * high, 128 * (high + 1), 16)
            items = [values[t][l : l + 16, :] for l in levels]
            for b, item in enumerate(exchange_lanes(items, 16)):
                start = 160 * (8 * (t % 2) + b) + 2 * (t // 2) + high
                rows[pl.ds(start, 16, stride=10), :] = item
    out[...] = rows[...].astype(BF16)


def final_kernel(
    truncation, band, slot_pair, lane_latitude, weights, received, legendre, out, rows, full_out, sent
):
    width = legendre.shape[1]
    rows[...] = received[...].astype(F32)
    target = lax.broadcasted_iota(jnp.int32, (256, 256), 0)
    lane = lax.broadcasted_iota(jnp.int32, (256, 256), 1)
    source = lane_latitude[...]
    wave = ((target >> 5) << 1) | (target & 1)
    turn = ((lane >> 4 == ((target >> 1) & 15)) & ((lane & 15) == wave)).astype(F32).astype(BF16)
    value = jnp.where((target >= 128) & (source >= 128), F32(-1.0), F32(1.0))
    fold = jnp.where((target & 127) == (source & 127), value, 0.0).astype(BF16)
    doubled = jnp.concatenate([weights[...], weights[...]], 1)
    parts = []
    for g in range(GROUPS):
        halves = [rows[pl.ds(2 * g + h, 256, stride=10), :].astype(BF16) for h in (0, 1)]
        turned = dot(turn, jnp.concatenate(halves, 1), NT).astype(BF16)
        parts.append((dot(turned, fold, NT) * doubled).astype(BF16))
    copies = []
    for g in range(GROUPS):
        for s in range(4):
            slot = 4 * g + s
            own = parts[g][64 * s : 64 * (s + 1)]
            left = jnp.concatenate([own[:, :128], own[:, 128:]], 0)
            full = dot(left, legendre[slot], NT)
            first, odd = slot_columns(slot_pair[band[0] * 20 + slot], width, truncation)
            even_part = jnp.where(first, full[0:32], full[32:64])
            odd_part = jnp.where(first, full[64:96], full[96:128])
            chosen = jnp.where(odd == 0, even_part, odd_part)
            full_out[:, slot] = chosen.reshape(16, 2, width)
        cut = pl.ds(4 * g, 4)
        copies.append(pltpu.make_async_copy(full_out.at[:, cut], out.at[:, cut], sent.at[g]))
        copies[g].start()
    for copy in copies:
        copy.wait()


def whole(shape):
    return pl.BlockSpec(shape, lambda i: (0,) * len(shape))


SMEM = pl.BlockSpec(memory_space=pltpu.SMEM)
VMEM = pl.BlockSpec(memory_space=pltpu.VMEM)
HBM = pl.BlockSpec(memory_space=pltpu.HBM)


def cost(flops, size):
    return pl.CostEstimate(flops=flops, bytes_accessed=size, transcendentals=0)


def in_hbm(array):
    return pltpu.with_memory_space_constraint(array, pltpu.HBM)


def everywhere(message):
    pieces = message.reshape(ROWS // 2, 2, 128)
    pieces = lax.all_to_all(pieces, ("band", "lev"), split_axis=0, concat_axis=0, tiled=True)
    return pieces.reshape(ROWS, 128)


def per_device(
    spectral, legendre, weights, vertical, grid_factor, points, cutoffs, row_latitude, slot_pair
):
    band = lax.axis_index("band").astype(jnp.int32).reshape(1)
    truncation = 2 * slot_pair.shape[0] - 1
    width = spectral.shape[3]
    row_width = grid_factor.shape[1]
    by_slot = spectral.transpose(0, 2, 1, 3)
    legendre = legendre.transpose(0, 2, 1)
    lane_latitude = row_latitude.reshape(1, 256)
    pairs = slot_pair.reshape(NB, GROUPS, 4).transpose(1, 0, 2)
    waves = jnp.stack([pairs, truncation - pairs], -1)
    waves = jnp.broadcast_to(waves[..., None], waves.shape + (2,)).reshape(1, WAVES).astype(F32)

    message = pl.pallas_call(
        lambda *refs: send_kernel(truncation, *refs),
        in_specs=[SMEM, HBM, HBM, HBM, HBM],
        out_specs=HBM,
        out_shape=pltpu.HBM((NB, GROUPS, 16, 256), BF16),
        scratch_shapes=[
            pltpu.VMEM((GROUPS, 256, 256), BF16),
            pltpu.VMEM((GROUPS, 2, 256, 128), F32),
            pltpu.VMEM(by_slot.shape, BF16),
            pltpu.VMEM(legendre.shape, BF16),
            pltpu.VMEM((NB, GROUPS, 16, 256), BF16),
            pltpu.SMEM(slot_pair.shape, jnp.int32),
            pltpu.VMEM((1, 256), jnp.int32),
            pltpu.SemaphoreType.DMA((GROUPS + 3,)),
            pltpu.SemaphoreType.DMA((GROUPS,)),
        ],
        compiler_params=params(),
        cost_estimate=cost(2 * 20 * 128 * 768 * 128, 5_000_000),
        name="legendre_send",
    )(band, in_hbm(slot_pair), in_hbm(lane_latitude), in_hbm(by_slot), in_hbm(legendre))
    received = lax.all_to_all(message, "band", split_axis=0, concat_axis=0, tiled=True)

    per_step = 2
    table, outer_cos, outer_sin = pl.pallas_call(
        lambda *refs: table_kernel(per_step, *refs),
        grid=(NB // per_step,),
        in_specs=[SMEM, SMEM, SMEM, whole((1, WAVES))],
        out_specs=[
            pl.BlockSpec((per_step, 256, WAVES), lambda i: (i, 0, 0)),
            pl.BlockSpec((per_step, 16, WAVES), lambda i: (i, 0, 0)),
            pl.BlockSpec((per_step, 16, WAVES), lambda i: (i, 0, 0)),
        ],
        out_shape=[
            pltpu.HBM((NB, 256, WAVES), BF16),
            jax.ShapeDtypeStruct((NB, 16, WAVES), F32),
            jax.ShapeDtypeStruct((NB, 16, WAVES), F32),
        ],
        scratch_shapes=[pltpu.VMEM((4, 16, WAVES), F32)],
        compiler_params=params(),
        cost_estimate=cost(16 * 256 * 1280 * 20, 14_000_000),
        name="phase_tables",
    )(band, row_latitude, points, waves)

    per_step = 4
    factor = grid_factor.astype(F32).reshape(NB, 1, row_width)
    grid_field, harmonic = pl.pallas_call(
        lambda *refs: rows_kernel(per_step, *refs),
        grid=(NB // per_step,),
        in_specs=[
            SMEM, SMEM, SMEM, SMEM,
            whole((NB, GROUPS, 16, 256)),
            whole((1, WAVES)),
            pl.BlockSpec((per_step, 256, WAVES), lambda i: (i, 0, 0)),
            pl.BlockSpec((per_step, 16, WAVES), lambda i: (i, 0, 0)),
            pl.BlockSpec((per_step, 16, WAVES), lambda i: (i, 0, 0)),
            pl.BlockSpec((per_step, 1, row_width), lambda i: (i, 0, 0)),
        ],
        out_specs=[
            pl.BlockSpec((per_step, 16, row_width), lambda i: (i, 0, 0)),
            pl.BlockSpec((per_step, 16, WAVES), lambda i: (i, 0, 0)),
        ],
        out_shape=[
            jax.ShapeDtypeStruct((NB, 16, row_width), BF16),
            jax.ShapeDtypeStruct((NB, 16, WAVES), BF16),
        ],
        scratch_shapes=[
            pltpu.VMEM((NB, 16, WAVES), F32),
            pltpu.VMEM((per_step, 176, WAVES), BF16),
            pltpu.VMEM((per_step, 176, 256), BF16),
        ],
        compiler_params=params(32),
        cost_estimate=cost(4 * 16 * 176 * 1280 * 256, 17_000_000),
        name="grid_rows",
    )(band, row_latitude, points, cutoffs, received, waves, in_hbm(table), outer_cos, outer_sin,
      factor)

    levels_in = lax.all_to_all(harmonic, "lev", split_axis=0, concat_axis=0, tiled=True)
    outgoing = pl.pallas_call(
        mix_kernel,
        in_specs=[VMEM, VMEM],
        out_specs=VMEM,
        out_shape=jax.ShapeDtypeStruct((ROWS, 128), BF16),
        scratch_shapes=[pltpu.VMEM((ROWS, 128), F32)],
        compiler_params=params(),
        cost_estimate=cost(2 * 256 * 256 * 1280, 1_400_000),
        name="vertical_mix",
    )(vertical, levels_in)
    returned = everywhere(outgoing)

    round_trip = pl.pallas_call(
        lambda *refs: final_kernel(truncation, *refs),
        in_specs=[SMEM, SMEM, VMEM, VMEM, VMEM, VMEM],
        out_specs=HBM,
        out_shape=jax.ShapeDtypeStruct((16, 20, 2, width), F32),
        scratch_shapes=[
            pltpu.VMEM((ROWS, 128), F32),
            pltpu.VMEM((16, 20, 2, width), F32),
            pltpu.SemaphoreType.DMA((GROUPS,)),
        ],
        compiler_params=params(),
        cost_estimate=cost(2 * 20 * 128 * 768 * 128, 6_000_000),
        name="legendre_return",
    )(
        band, slot_pair, lane_latitude, weights.reshape(1, 128), returned, legendre,
    )
    return (grid_field, round_trip.transpose(0, 2, 1, 3))


def solution(mesh):
    in_specs = (
        P("lev", None, "band", None),
        P("band", None, None),
        P(),
        P(),
        P("band", None),
        P(),
        P(),
        P(),
        P(),
    )
    out_specs = (P("band", "lev", None), P("lev", None, "band", None))
    return jax.shard_map(
        per_device, mesh=mesh, in_specs=in_specs, out_specs=out_specs, check_vma=False
    )
```

```python
import math

import jax
import jax.numpy as jnp
from jax import lax
from jax.experimental import pallas as pl
from jax.experimental.pallas import tpu as pltpu
from jax.sharding import PartitionSpec as P

F32, BF16 = jnp.float32, jnp.bfloat16
NB = 16
GROUPS = 5
ROWS = 2560
WAVES = 1280
HALF = 640
COS = (1.0, -19.739208221435547, 64.93938446044922, -85.45658111572266,
       60.241241455078125, -26.39919662475586, 7.783571243286133, -1.4335278272628784)
SIN = (6.2831854820251465, -41.34170150756836, 81.6052474975586, -76.70577239990234,
       42.05741882324219, -15.084507942199707, 3.775092124938965, -0.6134149432182312)
NT = (((1,), (1,)), ((), ()))


def params(limit=24):
    return pltpu.CompilerParams(vmem_limit_bytes=limit * 1024 * 1024)


def dot(a, b, dims=(((1,), (0,)), ((), ()))):
    return lax.dot_general(a, b, dims, preferred_element_type=F32)


def exchange_chunks(items, width):
    items = list(items)
    lane = lax.broadcasted_iota(jnp.int32, items[0][0].shape, 1)
    for level in range(4):
        step = 1 << level
        shift = width * step
        for low in range(16):
            if low & step:
                continue
            a, b = items[low], items[low + step]
            if shift == 128:
                items[low], items[low + step] = (a[0], b[0]), (a[1], b[1])
                continue
            keep = (lane & shift) == 0
            items[low] = tuple(jnp.where(keep, a[h], pltpu.roll(b[h], shift, 1)) for h in (0, 1))
            items[low + step] = tuple(
                jnp.where(keep, pltpu.roll(a[h], 128 - shift, 1), b[h]) for h in (0, 1)
            )
    return items


def exchange_lanes(items, width):
    items = list(items)
    lane = lax.broadcasted_iota(jnp.int32, items[0].shape, 1)
    count = len(items)
    for level in range(count.bit_length() - 1):
        step = 1 << level
        shift = width * step
        keep = (lane & shift) == 0
        for low in range(count):
            if low & step:
                continue
            a, b = items[low], items[low + step]
            items[low] = jnp.where(keep, a, pltpu.roll(b, shift, 1))
            items[low + step] = jnp.where(keep, pltpu.roll(a, 128 - shift, 1), b)
    return items


def slot_columns(pair, width, truncation):
    column = lax.broadcasted_iota(jnp.int32, (1, width), 1)
    split = truncation + 1 - pair
    first = column < split
    odd = jnp.where(first, column, column - split) & 1
    return first, odd


def table_kernel(
    rows_per_step, band, row_latitude, points, waves, table, outer_cos, outer_sin, seeds
):
    step = pl.program_id(0)
    wave = waves[...]
    for r in range(rows_per_step):
        lat = row_latitude[band[0] * NB + step * rows_per_step + r] & (points.shape[0] - 1)
        count = jnp.full((1, HALF), 2.0 * points[lat].astype(F32))
        inverse = 1.0 / count

        def circle(rows, stride, offset):
            index = lax.broadcasted_iota(jnp.int32, (rows, HALF), 0).astype(F32)
            product = wave * (index * stride + offset)
            turns = jnp.floor(product * inverse + 0.5)
            y = (product - turns * count) * inverse
            z = y * y
            c = jnp.full_like(z, COS[-1])
            s = jnp.full_like(z, SIN[-1])
            for k in range(6, -1, -1):
                c = c * z + COS[k]
                s = s * z + SIN[k]
            return c, s * y

        c1, s1 = circle(16, 2.0, 1.0)
        c2, s2 = circle(16, 32.0, 0.0)
        seeds[0] = c1
        seeds[1] = s1
        seeds[2] = c2
        seeds[3] = s2
        c3, s3 = circle(8, 1024.0, 511.0)
        outer_cos[r] = c3
        outer_sin[r] = s3
        for t in range(5):
            lanes = slice(128 * t, 128 * (t + 1))
            c1, s1 = seeds[0, :, lanes], seeds[1, :, lanes]
            for a in range(16):
                c2, s2 = seeds[2, a : a + 1, lanes], seeds[3, a : a + 1, lanes]
                rows = slice(16 * a, 16 * (a + 1))
                table[r, 0, rows, lanes] = (c2 * c1 - s2 * s1).astype(BF16)
                table[r, 1, rows, lanes] = (s2 * c1 + c2 * s1).astype(BF16)


def send_kernel(
    truncation, band, all_pairs, latitudes, spectral, legendre, out, sums, spread, spectral_in,
    legendre_in, messages, slot_pair, lane_latitude, ready, sent
):
    width = spectral.shape[-1]
    slots = pltpu.make_async_copy(all_pairs, slot_pair, ready.at[GROUPS + 1])
    slots.start()
    rows = pltpu.make_async_copy(latitudes, lane_latitude, ready.at[GROUPS + 2])
    rows.start()
    whole_spectral = pltpu.make_async_copy(spectral, spectral_in, ready.at[GROUPS])
    whole_spectral.start()
    copies = []
    for g in range(GROUPS):
        cut = pl.ds(4 * g, 4)
        copies.append(pltpu.make_async_copy(legendre.at[cut], legendre_in.at[cut], ready.at[g]))
        copies[g].start()
    index = lax.broadcasted_iota(jnp.int32, (256, 256), 0)
    rows.wait()
    place = (index == lane_latitude[...]).astype(F32).astype(BF16)
    slots.wait()
    whole_spectral.wait()
    for g in range(GROUPS):
        copies[g].wait()
        values = []
        for s in range(4 * g, 4 * g + 4):
            first, odd = slot_columns(slot_pair[band[0] * 20 + s], width, truncation)
            one = first.astype(F32)
            sign = 1.0 - 2.0 * odd.astype(F32)
            x = spectral_in[:, s].reshape(32, width)
            picks = [one, 1.0 - one, one * sign, (1.0 - one) * sign]
            left = jnp.concatenate([x * p.astype(BF16) for p in picks], 0)
            values.append(dot(left, legendre_in[s]).astype(BF16))
        for s in range(4):
            sums[g, 64 * s : 64 * (s + 1), :128] = values[s][:64]
            sums[g, 64 * s : 64 * (s + 1), 128:] = values[s][64:]
    for g in range(GROUPS):
        placed = dot(sums[g], place)
        spread[g, 0] = placed[:, :128]
        spread[g, 1] = placed[:, 128:]
        items = []
        for u in range(16):
            at = pl.ds(32 * (u & 7) + (u >> 3), 16, stride=2)
            items.append((spread[g, 0, at, :], spread[g, 1, at, :]))
        for b, (lo, hi) in enumerate(exchange_chunks(items, 16)):
            messages[b, g, :, :128] = lo.astype(BF16)
            messages[b, g, :, 128:] = hi.astype(BF16)
        cut = pl.ds(g, 1)
        copies[g] = pltpu.make_async_copy(messages.at[:, cut], out.at[:, cut], sent.at[g])
        copies[g].start()
    for copy in copies:
        copy.wait()


def rows_kernel(
    rows_per_step, band, row_latitude, points, cutoffs, received, waves, table, outer_cos,
    outer_sin, factor_left, factor_right, grid_field, out, fourier, twisted, samples
):
    step = pl.program_id(0)

    @pl.when(step == 0)
    def _():
        for g in range(GROUPS):
            items = []
            for src in range(NB):
                block = received[src, g].astype(F32)
                items.append((block[:, :128], block[:, 128:]))
            for row, parts in enumerate(exchange_chunks(items, 1)):
                for h in range(2):
                    fourier[row, h, :, 128 * g : 128 * (g + 1)] = parts[h]

    lane = lax.broadcasted_iota(jnp.int32, (1, 256), 1)
    backward = 127 - lax.broadcasted_iota(jnp.int32, (16, 128), 1)

    def limits(r):
        lat = row_latitude[band[0] * NB + step * rows_per_step + r] & (points.shape[0] - 1)
        return points[lat], cutoffs[lat].astype(F32)

    def twist(r):
        cutoff = limits(r)[1]
        for t in range(5):
            lanes = slice(128 * t, 128 * (t + 1))
            wave = waves[:, lanes]
            kept = (wave <= cutoff).astype(F32)
            weight = kept * jnp.where(wave == 0.0, F32(1.0), F32(2.0))
            real = fourier[step * rows_per_step + r, 0, :, lanes] * weight
            imag = fourier[step * rows_per_step + r, 1, :, lanes] * weight
            for b in range(6):
                cosine, sine = outer_cos[r, b : b + 1, lanes], outer_sin[r, b : b + 1, lanes]
                rows = slice(16 * b, 16 * (b + 1))
                twisted[r, 0, rows, lanes] = (real * cosine - imag * sine).astype(BF16)
                twisted[r, 1, rows, lanes] = (real * sine + imag * cosine).astype(BF16)

    def inverse(r):
        count = limits(r)[0]
        even = dot(twisted[r, 0], table[step * rows_per_step + r, 0], NT)
        odd = dot(twisted[r, 1], table[step * rows_per_step + r, 1], NT)
        for b in range(6):
            rows, lanes = slice(16 * b, 16 * (b + 1)), slice(256 * b, 256 * (b + 1))
            left = jnp.where(512 * b + 255 - lane < count, even[rows] + odd[rows], 0.0)
            for k in range(2 if b < 5 else 1):
                piece = left[:, 128:] if k == 0 else left[:, :128]
                turned = jnp.take_along_axis(piece, backward, axis=1).astype(BF16)
                at = 512 * b + 128 * k
                grid_field[r, :, at : at + 128] = turned
            left = left.astype(BF16).astype(F32) * factor_left[r, :, lanes]
            if b < 5:
                right = jnp.where(512 * b + 256 + lane < count, even[rows] - odd[rows], 0.0)
                right = right.astype(BF16)
                grid_field[r, :, 512 * b + 256 : 512 * b + 512] = right
                right = right.astype(F32) * factor_right[r, :, lanes]
                samples[r, 0, rows] = (right + left).astype(BF16)
                samples[r, 1, rows] = (right - left).astype(BF16)
            else:
                samples[r, 0, rows] = left.astype(BF16)
                samples[r, 1, rows] = (-left).astype(BF16)

    def direct(r):
        count, cutoff = limits(r)
        for start in range(0, HALF, 256):
            size = min(256, HALF - start)
            lanes = slice(start, start + size)
            even = dot(samples[r, 0], table[step * rows_per_step + r, 0, :, lanes])
            odd = dot(samples[r, 1], table[step * rows_per_step + r, 1, :, lanes])
            real = jnp.zeros((16, size), F32)
            imag = jnp.zeros((16, size), F32)
            for b in range(6):
                rows = slice(16 * b, 16 * (b + 1))
                cosine, sine = outer_cos[r, b : b + 1, lanes], outer_sin[r, b : b + 1, lanes]
                real = real + (even[rows] * cosine - odd[rows] * sine)
                imag = imag + (even[rows] * sine + odd[rows] * cosine)
            kept = (waves[:, lanes] <= cutoff).astype(F32)
            scale = kept / jnp.full((1, size), count.astype(F32))
            real = (real * scale).astype(BF16)
            imag = (imag * -scale).astype(BF16)
            for k in range(size // 128):
                at, piece = 2 * (start + 128 * k), slice(128 * k, 128 * (k + 1))
                out[r, :, at : at + 128] = real[:, piece]
                out[r, :, at + 128 : at + 256] = imag[:, piece]

    twist(0)
    for r in range(rows_per_step):
        if r + 1 < rows_per_step:
            twist(r + 1)
        inverse(r)
        if r > 0:
            direct(r - 1)
    direct(rows_per_step - 1)


def mix_kernel(vertical, received, out, rows):
    index = lax.broadcasted_iota(jnp.int32, (256, 256), 0)
    lane = lax.broadcasted_iota(jnp.int32, (256, 256), 1)
    by_level = (((lane & 15) == index >> 4) & (lane >> 4 == (index & 15))).astype(F32).astype(BF16)
    matrix = dot(by_level, vertical[...]).astype(BF16)
    block = received[...].reshape(256, WAVES)
    values = []
    for t in range(5):
        value = dot(matrix, block[:, 256 * t : 256 * (t + 1)])
        values += [value[:, :128], value[:, 128:]]
    for t in range(10):
        items = [values[t][l : l + 16, :] for l in range(0, 256, 16)]
        for b, item in enumerate(exchange_lanes(items, 1)):
            rows[pl.ds(160 * b + t, 16, stride=10), :] = item
    out[...] = rows[...].astype(BF16)


def final_kernel(
    truncation, band, slot_pair, lane_latitude, weights, received, legendre, out, rows, full_out, sent
):
    width = legendre.shape[1]
    rows[...] = received[...].astype(F32)
    target = lax.broadcasted_iota(jnp.int32, (256, 256), 0)
    lane = lax.broadcasted_iota(jnp.int32, (256, 256), 1)
    source = lane_latitude[...]
    wave = ((target & 1) << 3) | (target >> 5)
    turn = ((lane >> 4 == wave) & ((lane & 15) == ((target >> 1) & 15))).astype(F32).astype(BF16)
    value = jnp.where((target >= 128) & (source >= 128), F32(-1.0), F32(1.0))
    fold = jnp.where((target & 127) == (source & 127), value, 0.0).astype(BF16)
    doubled = jnp.concatenate([weights[...], weights[...]], 1)
    parts = []
    for g in range(GROUPS):
        halves = [rows[pl.ds(2 * g + h, 256, stride=10), :].astype(BF16) for h in (0, 1)]
        turned = dot(turn, jnp.concatenate(halves, 1), NT).astype(BF16)
        parts.append((dot(turned, fold, NT) * doubled).astype(BF16))
    copies = []
    for g in range(GROUPS):
        for s in range(4):
            slot = 4 * g + s
            own = parts[g][64 * s : 64 * (s + 1)]
            left = jnp.concatenate([own[:, :128], own[:, 128:]], 0)
            full = dot(left, legendre[slot], NT)
            first, odd = slot_columns(slot_pair[band[0] * 20 + slot], width, truncation)
            even_part = jnp.where(first, full[0:32], full[32:64])
            odd_part = jnp.where(first, full[64:96], full[96:128])
            chosen = jnp.where(odd == 0, even_part, odd_part)
            full_out[:, slot] = chosen.reshape(16, 2, width)
        cut = pl.ds(4 * g, 4)
        copies.append(pltpu.make_async_copy(full_out.at[:, cut], out.at[:, cut], sent.at[g]))
        copies[g].start()
    for copy in copies:
        copy.wait()


def whole(shape):
    return pl.BlockSpec(shape, lambda i: (0,) * len(shape))


SMEM = pl.BlockSpec(memory_space=pltpu.SMEM)
VMEM = pl.BlockSpec(memory_space=pltpu.VMEM)
HBM = pl.BlockSpec(memory_space=pltpu.HBM)


def cost(flops, size):
    return pl.CostEstimate(flops=flops, bytes_accessed=size, transcendentals=0)


def in_hbm(array):
    return pltpu.with_memory_space_constraint(array, pltpu.HBM)


def everywhere(message):
    pieces = message.reshape(ROWS // 2, 2, 128)
    pieces = lax.all_to_all(pieces, ("band", "lev"), split_axis=0, concat_axis=0, tiled=True)
    return pieces.reshape(ROWS, 128)


def per_device(
    spectral, legendre, weights, vertical, grid_factor, points, cutoffs, row_latitude, slot_pair
):
    band = lax.axis_index("band").astype(jnp.int32).reshape(1)
    truncation = 2 * slot_pair.shape[0] - 1
    width = spectral.shape[3]
    row_width = grid_factor.shape[1]
    by_slot = spectral.transpose(0, 2, 1, 3)
    legendre = legendre.transpose(0, 2, 1)
    lane_latitude = row_latitude.reshape(1, 256)
    pairs = slot_pair.reshape(NB, GROUPS, 4).transpose(1, 2, 0)
    waves = jnp.stack([pairs, truncation - pairs], 2).reshape(1, HALF).astype(F32)

    message = pl.pallas_call(
        lambda *refs: send_kernel(truncation, *refs),
        in_specs=[SMEM, HBM, HBM, HBM, HBM],
        out_specs=HBM,
        out_shape=pltpu.HBM((NB, GROUPS, 16, 256), BF16),
        scratch_shapes=[
            pltpu.VMEM((GROUPS, 256, 256), BF16),
            pltpu.VMEM((GROUPS, 2, 256, 128), F32),
            pltpu.VMEM(by_slot.shape, BF16),
            pltpu.VMEM(legendre.shape, BF16),
            pltpu.VMEM((NB, GROUPS, 16, 256), BF16),
            pltpu.SMEM(slot_pair.shape, jnp.int32),
            pltpu.VMEM((1, 256), jnp.int32),
            pltpu.SemaphoreType.DMA((GROUPS + 3,)),
            pltpu.SemaphoreType.DMA((GROUPS,)),
        ],
        compiler_params=params(),
        cost_estimate=cost(2 * 20 * 128 * 768 * 128, 5_000_000),
        name="legendre_send",
    )(band, in_hbm(slot_pair), in_hbm(lane_latitude), in_hbm(by_slot), in_hbm(legendre))
    received = lax.all_to_all(message, "band", split_axis=0, concat_axis=0, tiled=True)

    per_step = 2
    table, outer_cos, outer_sin = pl.pallas_call(
        lambda *refs: table_kernel(per_step, *refs),
        grid=(NB // per_step,),
        in_specs=[SMEM, SMEM, SMEM, whole((1, HALF))],
        out_specs=[
            pl.BlockSpec((per_step, 2, 256, HALF), lambda i: (i, 0, 0, 0)),
            pl.BlockSpec((per_step, 8, HALF), lambda i: (i, 0, 0)),
            pl.BlockSpec((per_step, 8, HALF), lambda i: (i, 0, 0)),
        ],
        out_shape=[
            pltpu.VMEM((NB, 2, 256, HALF), BF16),
            jax.ShapeDtypeStruct((NB, 8, HALF), F32),
            jax.ShapeDtypeStruct((NB, 8, HALF), F32),
        ],
        scratch_shapes=[pltpu.VMEM((4, 16, HALF), F32)],
        compiler_params=params(),
        cost_estimate=cost(16 * 256 * 1280 * 20, 7_000_000),
        name="phase_tables",
    )(band, row_latitude, points, waves)

    per_step = 8
    factor = jnp.pad(grid_factor, ((0, 0), (0, 3072 - row_width))).reshape(NB, 6, 2, 256).astype(F32)
    factor_left = factor[:, :, 0, ::-1].reshape(NB, 1, 1536)
    factor_right = factor[:, :5, 1].reshape(NB, 1, 1280)
    grid_field, harmonic = pl.pallas_call(
        lambda *refs: rows_kernel(per_step, *refs),
        grid=(NB // per_step,),
        in_specs=[
            SMEM, SMEM, SMEM, SMEM,
            whole((NB, GROUPS, 16, 256)),
            whole((1, HALF)),
            VMEM,
            pl.BlockSpec((per_step, 8, HALF), lambda i: (i, 0, 0)),
            pl.BlockSpec((per_step, 8, HALF), lambda i: (i, 0, 0)),
            pl.BlockSpec((per_step, 1, 1536), lambda i: (i, 0, 0)),
            pl.BlockSpec((per_step, 1, 1280), lambda i: (i, 0, 0)),
        ],
        out_specs=[
            pl.BlockSpec((per_step, 16, row_width), lambda i: (i, 0, 0)),
            pl.BlockSpec((per_step, 16, WAVES), lambda i: (i, 0, 0)),
        ],
        out_shape=[
            jax.ShapeDtypeStruct((NB, 16, row_width), BF16),
            jax.ShapeDtypeStruct((NB, 16, WAVES), BF16),
        ],
        scratch_shapes=[
            pltpu.VMEM((NB, 2, 16, HALF), F32),
            pltpu.VMEM((per_step, 2, 96, HALF), BF16),
            pltpu.VMEM((per_step, 2, 96, 256), BF16),
        ],
        compiler_params=params(),
        cost_estimate=cost(4 * 16 * 176 * 1280 * 256, 17_000_000),
        name="grid_rows",
    )(band, row_latitude, points, cutoffs, received, waves, pltpu.with_memory_space_constraint(table, pltpu.VMEM), outer_cos, outer_sin,
      factor_left, factor_right)

    levels_in = lax.all_to_all(harmonic, "lev", split_axis=0, concat_axis=0, tiled=True)
    outgoing = pl.pallas_call(
        mix_kernel,
        in_specs=[VMEM, VMEM],
        out_specs=VMEM,
        out_shape=jax.ShapeDtypeStruct((ROWS, 128), BF16),
        scratch_shapes=[pltpu.VMEM((ROWS, 128), F32)],
        compiler_params=params(),
        cost_estimate=cost(2 * 256 * 256 * 1280, 1_400_000),
        name="vertical_mix",
    )(vertical, levels_in)
    returned = everywhere(outgoing)

    round_trip = pl.pallas_call(
        lambda *refs: final_kernel(truncation, *refs),
        in_specs=[SMEM, SMEM, VMEM, VMEM, VMEM, VMEM],
        out_specs=HBM,
        out_shape=jax.ShapeDtypeStruct((16, 20, 2, width), F32),
        scratch_shapes=[
            pltpu.VMEM((ROWS, 128), F32),
            pltpu.VMEM((16, 20, 2, width), F32),
            pltpu.SemaphoreType.DMA((GROUPS,)),
        ],
        compiler_params=params(),
        cost_estimate=cost(2 * 20 * 128 * 768 * 128, 6_000_000),
        name="legendre_return",
    )(
        band, slot_pair, lane_latitude, weights.reshape(1, 128), returned, legendre,
    )
    return (grid_field, round_trip.transpose(0, 2, 1, 3))


def solution(mesh):
    in_specs = (
        P("lev", None, "band", None),
        P("band", None, None),
        P(),
        P(),
        P("band", None),
        P(),
        P(),
        P(),
        P(),
    )
    out_specs = (P("band", "lev", None), P("lev", None, "band", None))
    return jax.shard_map(
        per_device, mesh=mesh, in_specs=in_specs, out_specs=out_specs, check_vma=False
    )
```

```python
import math

import jax
import jax.numpy as jnp
from jax import lax
from jax.experimental import pallas as pl
from jax.experimental.pallas import tpu as pltpu
from jax.sharding import PartitionSpec as P

F32, BF16 = jnp.float32, jnp.bfloat16
NB = 16
GROUPS = 5
ROWS = 2560
WAVES = 1280
HALF = 640
COS = (1.0, -19.739208221435547, 64.93938446044922, -85.45658111572266,
       60.241241455078125, -26.39919662475586, 7.783571243286133, -1.4335278272628784)
SIN = (6.2831854820251465, -41.34170150756836, 81.6052474975586, -76.70577239990234,
       42.05741882324219, -15.084507942199707, 3.775092124938965, -0.6134149432182312)
NT = (((1,), (1,)), ((), ()))


def params(limit=24):
    return pltpu.CompilerParams(vmem_limit_bytes=limit * 1024 * 1024)


def dot(a, b, dims=(((1,), (0,)), ((), ()))):
    return lax.dot_general(a, b, dims, preferred_element_type=F32)


def exchange_chunks(items, width):
    items = list(items)
    lane = lax.broadcasted_iota(jnp.int32, items[0][0].shape, 1)
    for level in range(4):
        step = 1 << level
        shift = width * step
        for low in range(16):
            if low & step:
                continue
            a, b = items[low], items[low + step]
            if shift == 128:
                items[low], items[low + step] = (a[0], b[0]), (a[1], b[1])
                continue
            keep = (lane & shift) == 0
            items[low] = tuple(jnp.where(keep, a[h], pltpu.roll(b[h], shift, 1)) for h in (0, 1))
            items[low + step] = tuple(
                jnp.where(keep, pltpu.roll(a[h], 128 - shift, 1), b[h]) for h in (0, 1)
            )
    return items


def exchange_lanes(items, width):
    items = list(items)
    lane = lax.broadcasted_iota(jnp.int32, items[0].shape, 1)
    count = len(items)
    for level in range(count.bit_length() - 1):
        step = 1 << level
        shift = width * step
        keep = (lane & shift) == 0
        for low in range(count):
            if low & step:
                continue
            a, b = items[low], items[low + step]
            items[low] = jnp.where(keep, a, pltpu.roll(b, shift, 1))
            items[low + step] = jnp.where(keep, pltpu.roll(a, 128 - shift, 1), b)
    return items


def slot_columns(pair, width, truncation):
    column = lax.broadcasted_iota(jnp.int32, (1, width), 1)
    split = truncation + 1 - pair
    first = column < split
    odd = jnp.where(first, column, column - split) & 1
    return first, odd


def table_kernel(
    rows_per_step, band, row_latitude, points, waves, table, outer_cos, outer_sin, seeds
):
    step = pl.program_id(0)
    wave = waves[...]
    for r in range(rows_per_step):
        lat = row_latitude[band[0] * NB + step * rows_per_step + r] & (points.shape[0] - 1)
        count = jnp.full((1, HALF), 2.0 * points[lat].astype(F32))
        inverse = 1.0 / count

        def circle(rows, stride, offset):
            index = lax.broadcasted_iota(jnp.int32, (rows, HALF), 0).astype(F32)
            product = wave * (index * stride + offset)
            turns = jnp.floor(product * inverse + 0.5)
            y = (product - turns * count) * inverse
            z = y * y
            c = jnp.full_like(z, COS[-1])
            s = jnp.full_like(z, SIN[-1])
            for k in range(6, -1, -1):
                c = c * z + COS[k]
                s = s * z + SIN[k]
            return c, s * y

        c1, s1 = circle(16, 2.0, 1.0)
        c2, s2 = circle(8, 32.0, 0.0)
        seeds[0] = c1
        seeds[1] = s1
        seeds[2, :8] = c2
        seeds[3, :8] = s2
        c3, s3 = circle(16, 512.0, 255.0)
        outer_cos[r] = c3
        outer_sin[r] = s3
        for t in range(5):
            lanes = slice(128 * t, 128 * (t + 1))
            c1, s1 = seeds[0, :, lanes], seeds[1, :, lanes]
            for a in range(8):
                c2, s2 = seeds[2, a : a + 1, lanes], seeds[3, a : a + 1, lanes]
                rows = slice(16 * a, 16 * (a + 1))
                table[r, 0, rows, lanes] = (c2 * c1 - s2 * s1).astype(BF16)
                table[r, 1, rows, lanes] = (s2 * c1 + c2 * s1).astype(BF16)


def send_kernel(
    truncation, band, all_pairs, latitudes, spectral, legendre, out, sums, spread, spectral_in,
    legendre_in, messages, slot_pair, lane_latitude, ready, sent
):
    width = spectral.shape[-1]
    slots = pltpu.make_async_copy(all_pairs, slot_pair, ready.at[GROUPS + 1])
    slots.start()
    rows = pltpu.make_async_copy(latitudes, lane_latitude, ready.at[GROUPS + 2])
    rows.start()
    whole_spectral = pltpu.make_async_copy(spectral, spectral_in, ready.at[GROUPS])
    whole_spectral.start()
    copies = []
    for g in range(GROUPS):
        cut = pl.ds(4 * g, 4)
        copies.append(pltpu.make_async_copy(legendre.at[cut], legendre_in.at[cut], ready.at[g]))
        copies[g].start()
    index = lax.broadcasted_iota(jnp.int32, (256, 256), 0)
    rows.wait()
    place = (index == lane_latitude[...]).astype(F32).astype(BF16)
    slots.wait()
    whole_spectral.wait()
    for g in range(GROUPS):
        copies[g].wait()
        values = []
        for s in range(4 * g, 4 * g + 4):
            first, odd = slot_columns(slot_pair[band[0] * 20 + s], width, truncation)
            one = first.astype(F32)
            sign = 1.0 - 2.0 * odd.astype(F32)
            x = spectral_in[:, s].reshape(32, width)
            picks = [one, 1.0 - one, one * sign, (1.0 - one) * sign]
            left = jnp.concatenate([x * p.astype(BF16) for p in picks], 0)
            values.append(dot(left, legendre_in[s]).astype(BF16))
        for s in range(4):
            sums[g, 64 * s : 64 * (s + 1), :128] = values[s][:64]
            sums[g, 64 * s : 64 * (s + 1), 128:] = values[s][64:]
    for g in range(GROUPS):
        placed = dot(sums[g], place)
        spread[g, 0] = placed[:, :128]
        spread[g, 1] = placed[:, 128:]
        items = []
        for u in range(16):
            at = pl.ds(32 * (u & 7) + (u >> 3), 16, stride=2)
            items.append((spread[g, 0, at, :], spread[g, 1, at, :]))
        for b, (lo, hi) in enumerate(exchange_chunks(items, 16)):
            messages[b, g, :, :128] = lo.astype(BF16)
            messages[b, g, :, 128:] = hi.astype(BF16)
        cut = pl.ds(g, 1)
        copies[g] = pltpu.make_async_copy(messages.at[:, cut], out.at[:, cut], sent.at[g])
        copies[g].start()
    for copy in copies:
        copy.wait()


def rows_kernel(
    rows_per_step, band, row_latitude, points, cutoffs, received, waves, table, outer_cos,
    outer_sin, factor_left, factor_right, grid_field, out, fourier, twisted, samples
):
    step = pl.program_id(0)

    @pl.when(step == 0)
    def _():
        for g in range(GROUPS):
            items = []
            for src in range(NB):
                block = received[src, g].astype(F32)
                items.append((block[:, :128], block[:, 128:]))
            for row, parts in enumerate(exchange_chunks(items, 1)):
                for h in range(2):
                    fourier[row, h, :, 128 * g : 128 * (g + 1)] = parts[h]

    lane = lax.broadcasted_iota(jnp.int32, (1, 128), 1)
    backward = 127 - lax.broadcasted_iota(jnp.int32, (16, 128), 1)

    def limits(r):
        lat = row_latitude[band[0] * NB + step * rows_per_step + r] & (points.shape[0] - 1)
        return points[lat], cutoffs[lat].astype(F32)

    def twist(r):
        cutoff = limits(r)[1]
        for t in range(5):
            lanes = slice(128 * t, 128 * (t + 1))
            wave = waves[:, lanes]
            kept = (wave <= cutoff).astype(F32)
            weight = kept * jnp.where(wave == 0.0, F32(1.0), F32(2.0))
            real = fourier[step * rows_per_step + r, 0, :, lanes] * weight
            imag = fourier[step * rows_per_step + r, 1, :, lanes] * weight
            for b in range(11):
                cosine, sine = outer_cos[r, b : b + 1, lanes], outer_sin[r, b : b + 1, lanes]
                rows = slice(16 * b, 16 * (b + 1))
                twisted[r, 0, rows, lanes] = (real * cosine - imag * sine).astype(BF16)
                twisted[r, 1, rows, lanes] = (real * sine + imag * cosine).astype(BF16)

    def inverse(r):
        count = limits(r)[0]
        even = dot(twisted[r, 0], table[r, 0], NT)
        odd = dot(twisted[r, 1], table[r, 1], NT)
        for b in range(11):
            rows, lanes = slice(16 * b, 16 * (b + 1)), slice(128 * b, 128 * (b + 1))
            left = jnp.where(256 * b + 127 - lane < count, even[rows] + odd[rows], 0.0)
            turned = jnp.take_along_axis(left, backward, axis=1)
            grid_field[r, :, 256 * b : 256 * b + 128] = turned.astype(BF16)
            left = left.astype(BF16).astype(F32) * factor_left[r, :, lanes]
            if b < 10:
                right = jnp.where(256 * b + 128 + lane < count, even[rows] - odd[rows], 0.0)
                right = right.astype(BF16)
                grid_field[r, :, 256 * b + 128 : 256 * b + 256] = right
                right = right.astype(F32) * factor_right[r, :, lanes]
                samples[r, 0, rows] = (right + left).astype(BF16)
                samples[r, 1, rows] = (right - left).astype(BF16)
            else:
                samples[r, 0, rows] = left.astype(BF16)
                samples[r, 1, rows] = (-left).astype(BF16)

    def direct(r):
        count, cutoff = limits(r)
        for start in range(0, HALF, 256):
            size = min(256, HALF - start)
            lanes = slice(start, start + size)
            even = dot(samples[r, 0], table[r, 0, :, lanes])
            odd = dot(samples[r, 1], table[r, 1, :, lanes])
            real = jnp.zeros((16, size), F32)
            imag = jnp.zeros((16, size), F32)
            for b in range(11):
                rows = slice(16 * b, 16 * (b + 1))
                cosine, sine = outer_cos[r, b : b + 1, lanes], outer_sin[r, b : b + 1, lanes]
                real = real + (even[rows] * cosine - odd[rows] * sine)
                imag = imag + (even[rows] * sine + odd[rows] * cosine)
            kept = (waves[:, lanes] <= cutoff).astype(F32)
            scale = kept / jnp.full((1, size), count.astype(F32))
            real = (real * scale).astype(BF16)
            imag = (imag * -scale).astype(BF16)
            for k in range(size // 128):
                at, piece = 2 * (start + 128 * k), slice(128 * k, 128 * (k + 1))
                out[r, :, at : at + 128] = real[:, piece]
                out[r, :, at + 128 : at + 256] = imag[:, piece]

    twist(0)
    for r in range(rows_per_step):
        if r + 1 < rows_per_step:
            twist(r + 1)
        inverse(r)
        if r > 0:
            direct(r - 1)
    direct(rows_per_step - 1)


def mix_kernel(vertical, received, out, rows):
    index = lax.broadcasted_iota(jnp.int32, (256, 256), 0)
    lane = lax.broadcasted_iota(jnp.int32, (256, 256), 1)
    by_level = (((lane & 15) == index >> 4) & (lane >> 4 == (index & 15))).astype(F32).astype(BF16)
    matrix = dot(by_level, vertical[...]).astype(BF16)
    block = received[...].reshape(256, WAVES)
    values = []
    for t in range(5):
        value = dot(matrix, block[:, 256 * t : 256 * (t + 1)])
        values += [value[:, :128], value[:, 128:]]
    for t in range(10):
        items = [values[t][l : l + 16, :] for l in range(0, 256, 16)]
        for b, item in enumerate(exchange_lanes(items, 1)):
            rows[pl.ds(160 * b + t, 16, stride=10), :] = item
    out[...] = rows[...].astype(BF16)


def final_kernel(
    truncation, band, slot_pair, lane_latitude, weights, received, legendre, out, rows, full_out, sent
):
    width = legendre.shape[1]
    rows[...] = received[...].astype(F32)
    target = lax.broadcasted_iota(jnp.int32, (256, 256), 0)
    lane = lax.broadcasted_iota(jnp.int32, (256, 256), 1)
    source = lane_latitude[...]
    wave = ((target & 1) << 3) | (target >> 5)
    turn = ((lane >> 4 == wave) & ((lane & 15) == ((target >> 1) & 15))).astype(F32).astype(BF16)
    value = jnp.where((target >= 128) & (source >= 128), F32(-1.0), F32(1.0))
    fold = jnp.where((target & 127) == (source & 127), value, 0.0).astype(BF16)
    doubled = jnp.concatenate([weights[...], weights[...]], 1)
    parts = []
    for g in range(GROUPS):
        halves = [rows[pl.ds(2 * g + h, 256, stride=10), :].astype(BF16) for h in (0, 1)]
        turned = dot(turn, jnp.concatenate(halves, 1), NT).astype(BF16)
        parts.append((dot(turned, fold, NT) * doubled).astype(BF16))
    copies = []
    for g in range(GROUPS):
        for s in range(4):
            slot = 4 * g + s
            own = parts[g][64 * s : 64 * (s + 1)]
            left = jnp.concatenate([own[:, :128], own[:, 128:]], 0)
            full = dot(left, legendre[slot], NT)
            first, odd = slot_columns(slot_pair[band[0] * 20 + slot], width, truncation)
            even_part = jnp.where(first, full[0:32], full[32:64])
            odd_part = jnp.where(first, full[64:96], full[96:128])
            chosen = jnp.where(odd == 0, even_part, odd_part)
            full_out[:, slot] = chosen.reshape(16, 2, width)
        cut = pl.ds(4 * g, 4)
        copies.append(pltpu.make_async_copy(full_out.at[:, cut], out.at[:, cut], sent.at[g]))
        copies[g].start()
    for copy in copies:
        copy.wait()


def whole(shape):
    return pl.BlockSpec(shape, lambda i: (0,) * len(shape))


SMEM = pl.BlockSpec(memory_space=pltpu.SMEM)
VMEM = pl.BlockSpec(memory_space=pltpu.VMEM)
HBM = pl.BlockSpec(memory_space=pltpu.HBM)


def cost(flops, size):
    return pl.CostEstimate(flops=flops, bytes_accessed=size, transcendentals=0)


def in_hbm(array):
    return pltpu.with_memory_space_constraint(array, pltpu.HBM)


def everywhere(message):
    pieces = message.reshape(ROWS // 2, 2, 128)
    pieces = lax.all_to_all(pieces, ("band", "lev"), split_axis=0, concat_axis=0, tiled=True)
    return pieces.reshape(ROWS, 128)


def per_device(
    spectral, legendre, weights, vertical, grid_factor, points, cutoffs, row_latitude, slot_pair
):
    band = lax.axis_index("band").astype(jnp.int32).reshape(1)
    truncation = 2 * slot_pair.shape[0] - 1
    width = spectral.shape[3]
    row_width = grid_factor.shape[1]
    by_slot = spectral.transpose(0, 2, 1, 3)
    legendre = legendre.transpose(0, 2, 1)
    lane_latitude = row_latitude.reshape(1, 256)
    pairs = slot_pair.reshape(NB, GROUPS, 4).transpose(1, 2, 0)
    waves = jnp.stack([pairs, truncation - pairs], 2).reshape(1, HALF).astype(F32)

    message = pl.pallas_call(
        lambda *refs: send_kernel(truncation, *refs),
        in_specs=[SMEM, HBM, HBM, HBM, HBM],
        out_specs=HBM,
        out_shape=pltpu.HBM((NB, GROUPS, 16, 256), BF16),
        scratch_shapes=[
            pltpu.VMEM((GROUPS, 256, 256), BF16),
            pltpu.VMEM((GROUPS, 2, 256, 128), F32),
            pltpu.VMEM(by_slot.shape, BF16),
            pltpu.VMEM(legendre.shape, BF16),
            pltpu.VMEM((NB, GROUPS, 16, 256), BF16),
            pltpu.SMEM(slot_pair.shape, jnp.int32),
            pltpu.VMEM((1, 256), jnp.int32),
            pltpu.SemaphoreType.DMA((GROUPS + 3,)),
            pltpu.SemaphoreType.DMA((GROUPS,)),
        ],
        compiler_params=params(),
        cost_estimate=cost(2 * 20 * 128 * 768 * 128, 5_000_000),
        name="legendre_send",
    )(band, in_hbm(slot_pair), in_hbm(lane_latitude), in_hbm(by_slot), in_hbm(legendre))
    received = lax.all_to_all(message, "band", split_axis=0, concat_axis=0, tiled=True)

    per_step = 2
    table, outer_cos, outer_sin = pl.pallas_call(
        lambda *refs: table_kernel(per_step, *refs),
        grid=(NB // per_step,),
        in_specs=[SMEM, SMEM, SMEM, whole((1, HALF))],
        out_specs=[
            pl.BlockSpec((per_step, 2, 128, HALF), lambda i: (i, 0, 0, 0)),
            pl.BlockSpec((per_step, 16, HALF), lambda i: (i, 0, 0)),
            pl.BlockSpec((per_step, 16, HALF), lambda i: (i, 0, 0)),
        ],
        out_shape=[
            pltpu.HBM((NB, 2, 128, HALF), BF16),
            jax.ShapeDtypeStruct((NB, 16, HALF), F32),
            jax.ShapeDtypeStruct((NB, 16, HALF), F32),
        ],
        scratch_shapes=[pltpu.VMEM((4, 16, HALF), F32)],
        compiler_params=params(),
        cost_estimate=cost(16 * 256 * 1280 * 20, 7_000_000),
        name="phase_tables",
    )(band, row_latitude, points, waves)

    per_step = 8
    factor = grid_factor.astype(F32).reshape(NB, row_width // 128, 128)
    factor_left = factor[:, 0::2, ::-1].reshape(NB, 1, 1408)
    factor_right = factor[:, 1::2].reshape(NB, 1, 1280)
    grid_field, harmonic = pl.pallas_call(
        lambda *refs: rows_kernel(per_step, *refs),
        grid=(NB // per_step,),
        in_specs=[
            SMEM, SMEM, SMEM, SMEM,
            whole((NB, GROUPS, 16, 256)),
            whole((1, HALF)),
            pl.BlockSpec((per_step, 2, 128, HALF), lambda i: (i, 0, 0, 0)),
            pl.BlockSpec((per_step, 16, HALF), lambda i: (i, 0, 0)),
            pl.BlockSpec((per_step, 16, HALF), lambda i: (i, 0, 0)),
            pl.BlockSpec((per_step, 1, 1408), lambda i: (i, 0, 0)),
            pl.BlockSpec((per_step, 1, 1280), lambda i: (i, 0, 0)),
        ],
        out_specs=[
            pl.BlockSpec((per_step, 16, row_width), lambda i: (i, 0, 0)),
            pl.BlockSpec((per_step, 16, WAVES), lambda i: (i, 0, 0)),
        ],
        out_shape=[
            jax.ShapeDtypeStruct((NB, 16, row_width), BF16),
            jax.ShapeDtypeStruct((NB, 16, WAVES), BF16),
        ],
        scratch_shapes=[
            pltpu.VMEM((NB, 2, 16, HALF), F32),
            pltpu.VMEM((per_step, 2, 176, HALF), BF16),
            pltpu.VMEM((per_step, 2, 176, 128), BF16),
        ],
        compiler_params=params(32),
        cost_estimate=cost(4 * 16 * 176 * 1280 * 256, 17_000_000),
        name="grid_rows",
    )(band, row_latitude, points, cutoffs, received, waves, in_hbm(table), outer_cos, outer_sin,
      factor_left, factor_right)

    levels_in = lax.all_to_all(harmonic, "lev", split_axis=0, concat_axis=0, tiled=True)
    outgoing = pl.pallas_call(
        mix_kernel,
        in_specs=[VMEM, VMEM],
        out_specs=VMEM,
        out_shape=jax.ShapeDtypeStruct((ROWS, 128), BF16),
        scratch_shapes=[pltpu.VMEM((ROWS, 128), F32)],
        compiler_params=params(),
        cost_estimate=cost(2 * 256 * 256 * 1280, 1_400_000),
        name="vertical_mix",
    )(vertical, levels_in)
    returned = everywhere(outgoing)

    round_trip = pl.pallas_call(
        lambda *refs: final_kernel(truncation, *refs),
        in_specs=[SMEM, SMEM, VMEM, VMEM, VMEM, VMEM],
        out_specs=HBM,
        out_shape=jax.ShapeDtypeStruct((16, 20, 2, width), F32),
        scratch_shapes=[
            pltpu.VMEM((ROWS, 128), F32),
            pltpu.VMEM((16, 20, 2, width), F32),
            pltpu.SemaphoreType.DMA((GROUPS,)),
        ],
        compiler_params=params(),
        cost_estimate=cost(2 * 20 * 128 * 768 * 128, 6_000_000),
        name="legendre_return",
    )(
        band, slot_pair, lane_latitude, weights.reshape(1, 128), returned, legendre,
    )
    return (grid_field, round_trip.transpose(0, 2, 1, 3))


def solution(mesh):
    in_specs = (
        P("lev", None, "band", None),
        P("band", None, None),
        P(),
        P(),
        P("band", None),
        P(),
        P(),
        P(),
        P(),
    )
    out_specs = (P("band", "lev", None), P("lev", None, "band", None))
    return jax.shard_map(
        per_device, mesh=mesh, in_specs=in_specs, out_specs=out_specs, check_vma=False
    )
```
